512 devices in a mesh: shot: 32 (over z_hi, x, core), sub: 16 (over z_lo, y).
Axes of the slice: x: 4, y: 8, z: 8 (z_hi: 4, z_lo: 2; z = z_hi * 2 + z_lo), core: 2. Of those that a mesh axis runs over, the one named last changes fastest.
Arguments:
- wave_before: bfloat16 [32, 128, 64, 128], P('shot', 'sub'), may hold values from -6 to 6
- wave_now: bfloat16 [32, 128, 64, 128], P('shot', 'sub'), may hold values from -6 to 6
- adjoint_before: bfloat16 [32, 128, 64, 128], P('shot', 'sub'), may hold values from -6 to 6
- adjoint_now: bfloat16 [32, 128, 64, 128], P('shot', 'sub'), may hold values from -6 to 6
- velocity: float32 [128, 64, 128], P('sub', 'shot'), may hold values from 0.06 to 0.19
- target_model: float32 [128, 64, 128], P('sub', 'shot'), may hold values from -0.8 to 1
- source_cell: int32 [32, 3], P('shot'), may hold values from 0 to 127, as said below
- source_wave: float32 [32, 2], P('shot'), may hold values from -12 to 12
- receiver_cell: int32 [32, 256, 2], P('shot'), may hold values from 0 to 127, as said below
- receiver_trace: float32 [32, 2, 256], P('shot'), may hold values from -10 to 10
- first_kernel: float32 [16, 2, 3, 3, 3], replicated, may hold values from -0.36 to 0.36
- first_bias: float32 [16], replicated, may hold values from -3 to 3
- second_kernel: float32 [1, 16, 3, 3, 3], replicated, may hold values from -0.9 to 0.9
- second_bias: float32 [1], replicated, may hold values from -4 to 4
Outputs:
- next_wave: bfloat16 [32, 128, 64, 128], P('shot', 'sub')
- new_velocity: float32 [128, 64, 128], P('sub', 'shot')
- first_kernel_move: float32 [16, 2, 3, 3, 3], replicated
- first_bias_move: float32 [16], replicated
- second_kernel_move: float32 [1, 16, 3, 3, 3], replicated
- second_bias_move: float32 [1], replicated
The draws below stay inside these ranges and needn't reach their ends.
Inputs may be any that keep to these rules, and one draw needn't show every extreme that they name: `source_cell`: row s holds shot s's source cell: a first index below 128, a second below 64, a third below 128. `receiver_cell`: entry [s, r] holds receiver r of shot s: a first index below 128 and a second below 64; several receivers may share a cell.
All inputs are finite; a program needn't handle non-finite values.
Results may differ from the reference program's by a relative error of at most 0.001.
Values sent between devices are 32-bit elements; how exact they have to be, the bound alone decides.
A program may use at most 128 MiB of HBM per device.

```python
import jax
import jax.numpy as jnp
from jax import lax

CH = 16
NZ = 128
NREC = 256
STEPS = 2
ZREC = 2
SHOTS = 32
NX = 128
NY = 64


def draw_source_cell(key, part):
    key = jax.random.fold_in(key, 5)
    streams = jax.random.split(key, 3)
    column_x = jax.random.randint(streams[0], (SHOTS,), 0, NX, dtype=jnp.int32)
    column_y = jax.random.randint(streams[1], (SHOTS,), 0, NY, dtype=jnp.int32)
    column_z = jax.random.randint(streams[2], (SHOTS,), 0, NZ, dtype=jnp.int32)
    column_x = column_x.at[0].set(NX - 1)
    column_y = column_y.at[1].set(NY - 1)
    column_z = column_z.at[2].set(NZ - 1)
    return jnp.stack([column_x, column_y, column_z], axis=1)


def draw_receiver_cell(key, part):
    key = jax.random.fold_in(key, 9)
    streams = jax.random.split(key, 2)
    column_x = jax.random.randint(streams[0], (SHOTS, NREC), 0, NX, dtype=jnp.int32)
    column_y = jax.random.randint(streams[1], (SHOTS, NREC), 0, NY, dtype=jnp.int32)
    column_x = column_x.at[0, 0].set(NX - 1)
    column_y = column_y.at[0, 1].set(NY - 1)
    return jnp.stack([column_x, column_y], axis=2)


def block_scale(key, shape, cuts, low, high):
    def one(dim, parts):
        draws = jax.random.uniform(jax.random.fold_in(jax.random.fold_in(key, 6), dim), (parts,), jnp.float32, low / len(cuts), high / len(cuts))
        return jnp.repeat(jnp.exp(draws), shape[dim] // parts).reshape((-1,) + (1,) * (len(shape) - dim - 1))

    loudness = one(*cuts[0])
    for cut in cuts[1:]:
        loudness = loudness * one(*cut)
    return loudness


def bell_draw(key, dims, scale, limit, pieces=(), kind=jnp.bfloat16):
    loudness = block_scale(key, dims, pieces, -0.22, 0.18) if pieces else 1.0
    array = jax.random.normal(key, dims, jnp.float32) * scale * loudness
    return jnp.minimum(jnp.maximum(array, -limit), limit).astype(kind)


def setup_inputs(seed: int = 0) -> dict:
    seeds = jax.random.split(jax.random.key(seed), 15)
    return {
        "wave_before": bell_draw(seeds[0], (SHOTS, NX, NY, NZ), 1.0, 6.0, ((0, 32), (1, 16))),
        "wave_now": bell_draw(seeds[1], (SHOTS, NX, NY, NZ), 1.0, 6.0, ((0, 32), (1, 16))),
        "adjoint_before": bell_draw(seeds[2], (SHOTS, NX, NY, NZ), 1.0, 6.0, ((0, 32), (1, 16))),
        "adjoint_now": bell_draw(seeds[3], (SHOTS, NX, NY, NZ), 1.0, 6.0, ((0, 32), (1, 16))),
        "velocity": jnp.clip(0.06 + 0.13 * jax.random.uniform(seeds[4], (NX, NY, NZ), jnp.float32) ** block_scale(seeds[4], (NX, NY, NZ), ((0, 16), (1, 32)), -0.2, 0.2), 0.06, 0.19),
        "target_model": jnp.clip(-0.8 + 1.8 * jax.random.uniform(seeds[5], (NX, NY, NZ), jnp.float32) ** block_scale(seeds[5], (NX, NY, NZ), ((0, 16), (1, 32)), -0.2, 0.2), -0.8, 1.0),
        "source_cell": draw_source_cell(jax.random.fold_in(seeds[14], 71), 0),
        "source_wave": bell_draw(seeds[7], (SHOTS, STEPS), 3.0, 12.0, ((0, 32),), jnp.float32),
        "receiver_cell": draw_receiver_cell(jax.random.fold_in(seeds[14], 71), 0),
        "receiver_trace": bell_draw(seeds[9], (SHOTS, STEPS, NREC), 2.0, 10.0, ((0, 32),), jnp.float32),
        "first_kernel": bell_draw(seeds[10], (CH, 2, 3, 3, 3), 0.06, 0.36, (), jnp.float32),
        "first_bias": bell_draw(seeds[11], (CH,), 0.5, 3.0, (), jnp.float32),
        "second_kernel": bell_draw(seeds[12], (1, CH, 3, 3, 3), 0.15, 0.9, (), jnp.float32),
        "second_bias": bell_draw(seeds[13], (1,), 1.0, 4.0, (), jnp.float32),
    }


COEFFS = (-205.0 / 72.0, 8.0 / 5.0, -1.0 / 5.0, 8.0 / 315.0, -1.0 / 560.0)
CENTER_SHIFT = 0.125
CENTER_GAIN = 16.0
NUMBERS = ('NCDHW', 'OIDHW', 'NCDHW')

def laplacian_inner(values):
    padded = jnp.pad(values, ((0, 0), (4, 4), (4, 4)))
    length = values.shape[0] - 8
    cols_y = values.shape[1]
    depth_z = values.shape[2]
    middle = padded[4:4 + length]
    running = 3.0 * COEFFS[0] * middle[:, 4:4 + cols_y, 4:4 + depth_z]
    for offset in range(1, 5):
        weight = COEFFS[offset]
        running = running + weight * (padded[4 + offset:4 + offset + length, 4:4 + cols_y, 4:4 + depth_z] + padded[4 - offset:4 - offset + length, 4:4 + cols_y, 4:4 + depth_z])
        running = running + weight * (middle[:, 4 + offset:4 + offset + cols_y, 4:4 + depth_z] + middle[:, 4 - offset:4 - offset + cols_y, 4:4 + depth_z])
        running = running + weight * (middle[:, 4:4 + cols_y, 4 + offset:4 + offset + depth_z] + middle[:, 4:4 + cols_y, 4 - offset:4 - offset + depth_z])
    return running

def laplacian(values):
    return laplacian_inner(jnp.pad(values, ((4, 4), (0, 0), (0, 0))))

def convolve(inputs, kernel, pads):
    return lax.conv_general_dilated(inputs, kernel, (1, 1, 1), pads, dimension_numbers=NUMBERS, precision=lax.Precision.HIGHEST)

def reference(wave_before, wave_now, adjoint_before, adjoint_now, velocity, target_model, source_cell, source_wave, receiver_cell, receiver_trace, first_kernel, first_bias, second_kernel, second_bias):

    def one_shot(running, shot_data):
        w_before, w_now, a_before, a_now, cell, amplitudes, rec_cells, traces = shot_data
        previous = w_before.astype(jnp.float32)
        current = w_now.astype(jnp.float32)
        lap_list = []
        for step in range(STEPS):
            lap_now = laplacian(current)
            fresh = 2.0 * current - previous + velocity * lap_now
            fresh = fresh.at[cell[0], cell[1], cell[2]].add(amplitudes[step])
            lap_list.append(lap_now)
            previous, current = (current, fresh)
        final_wave = current
        previous = a_before.astype(jnp.float32)
        current = a_now.astype(jnp.float32)
        adjoint_list = []
        for step in range(STEPS):
            lap_now = laplacian(current)
            surface = jnp.zeros((NX, NY), jnp.float32).at[rec_cells[:, 0], rec_cells[:, 1]].add(traces[step])
            fresh = 2.0 * current - previous + velocity * lap_now
            fresh = fresh.at[:, :, ZREC].add(surface)
            adjoint_list.append(fresh)
            previous, current = (current, fresh)
        shot_image = lap_list[0] * adjoint_list[STEPS - 1]
        for step in range(1, STEPS):
            shot_image = shot_image + lap_list[step] * adjoint_list[STEPS - 1 - step]
        return (running + shot_image, final_wave.astype(jnp.bfloat16))
    image_total, next_wave = lax.scan(one_shot, jnp.zeros((NX, NY, NZ), jnp.float32), (wave_before, wave_now, adjoint_before, adjoint_now, source_cell, source_wave, receiver_cell, receiver_trace))
    image = image_total * (1.0 / SHOTS)
    features = jnp.stack([image, (velocity - CENTER_SHIFT) * CENTER_GAIN])[None]

    def network(weights_one, offsets_one, weights_two, offsets_two):
        pre_act = convolve(features, weights_one, ((1, 1), (1, 1), (1, 1))) + offsets_one[None, :, None, None, None]
        hidden = jnp.tanh(pre_act)
        update = convolve(hidden, weights_two, ((1, 1), (1, 1), (1, 1)))[0, 0] + offsets_two[0]
        new_model = velocity - update
        misfit = new_model - target_model
        return (0.5 * jnp.sum(misfit * misfit), new_model)
    loss_sum, pullback, new_velocity = jax.vjp(network, first_kernel, first_bias, second_kernel, second_bias, has_aux=True)
    gradients = pullback(jnp.ones_like(loss_sum))
    square_sum = jnp.sum(gradients[0] * gradients[0]) + jnp.sum(gradients[1] * gradients[1]) + jnp.sum(gradients[2] * gradients[2]) + jnp.sum(gradients[3] * gradients[3])
    entries = first_kernel.size + first_bias.size + second_kernel.size + second_bias.size
    factor = 1.0 / jnp.sqrt(square_sum / entries + 1e-06)
    return (next_wave, new_velocity, gradients[0] * factor, gradients[1] * factor, gradients[2] * factor, gradients[3] * factor)
```

```python
import functools

import jax
import jax.numpy as jnp
from jax import lax
from jax.experimental import pallas as pl
from jax.experimental.pallas import tpu as pltpu
from jax.sharding import PartitionSpec as P

F32 = jnp.float32
BF16 = jnp.bfloat16
MESH = pl.DeviceIdType.MESH

ZREC = 2
COEFFS = (-205.0 / 72.0, 8.0 / 5.0, -1.0 / 5.0, 8.0 / 315.0, -1.0 / 560.0)
CENTER_SHIFT = 0.125
CENTER_GAIN = 16.0
ENTRIES = 1313

ROWS = 8
COLS = 64
DEPTH = 128
PAD = 8
N_SHOT, N_SUB = 32, 16
GRID_X, GRID_Y = 128, 64

TILES = 80
WIDE = 12
HID = 48 * DEPTH
CHUNK = 8 * DEPTH
OFFSETS = tuple(dy * WIDE + dx for dx in range(3) for dy in range(3))
BLOCKS = 10


def dot(a, b):
    return jnp.dot(a, b, preferred_element_type=F32)


def dot_t(a, b):
    return lax.dot_general(a, b, (((1,), (1,)), ((), ())), preferred_element_type=F32)


def halves(x):
    high = x.astype(BF16)
    return high, (x - high.astype(F32)).astype(BF16)


def shifted(x, dz):
    if dz == 0:
        return x
    z = lax.broadcasted_iota(jnp.int32, x.shape, 1)
    if dz > 0:
        return jnp.where(z < DEPTH - dz, pltpu.roll(x, DEPTH - dz, 1), 0.0)
    return jnp.where(z >= -dz, pltpu.roll(x, -dz, 1), 0.0)


def kernel(
    wb, wn, ab, an, vel, tgt, scell, swave, rcell, rtrace, wpack, b2,
    nw, nv, moves,
    p0, q0, p1, q1, lap0, imgacc, vfull, vg, surf, imgt, ra, acca, rb, hb_img, hb_vel,
    ext, gs, g2, rs, r2, fhi, flo, hid, smat, tt, mask, re,
    s_hal, r_hal, s_v1, r_v1, s_v2, r_v2, s_hv, r_hv, s_a, r_a, s_b, r_b, s_c, r_c, s_e, r_e,
):
    shot = lax.axis_index("shot")
    sub = lax.axis_index("sub")
    zh, xc = shot // 8, shot % 8
    zlo, yy = sub // 8, sub % 8
    zz = zh * 2 + zlo
    x0 = sub * ROWS
    up, down = (sub + 1) % N_SUB, (sub + N_SUB - 1) % N_SUB

    def xc_peer(k):
        return (zh * 8 + (xc + k) % 8, sub)

    def zh_peer(k):
        return (((zh + k) % 4) * 8 + xc, sub)

    def z_peer(k):
        z = (zz + k) % 8
        return ((z // 2) * 8 + xc, (z % 2) * 8 + yy)

    def y_peer(k):
        return (shot, zlo * 8 + (yy + k) % 8)

    def near(d, e):
        return ((shot + d + N_SHOT) % N_SHOT, (sub + e + N_SUB) % N_SUB)

    around = [(d, e) for d in (-1, 0, 1) for e in (-1, 0, 1) if (d, e) != (0, 0)]
    greeted = (
        [near(d, e) for d, e in around]
        + [xc_peer(k) for k in range(1, 8)]
        + [zh_peer(k) for k in range(1, 4)]
        + [z_peer(k) for k in range(1, 8)]
        + [y_peer(k) for k in range(1, 8)]
    )
    barrier = pltpu.get_barrier_semaphore()
    for device in greeted:
        pl.semaphore_signal(barrier, inc=1, device_id=device, device_id_type=MESH)

    pending = []

    def send(src, dst, ssem, rsem, device):
        copy = pltpu.make_async_remote_copy(
            src_ref=src, dst_ref=dst, send_sem=ssem, recv_sem=rsem, device_id=device, device_id_type=MESH
        )
        copy.start()
        pending.append(copy)
        return copy

    zeros_pad = jnp.zeros((16, PAD, DEPTH), F32)
    for field in (p0, q0, p1, q1):
        field[:, 0:PAD, :] = zeros_pad
        field[:, PAD + COLS :, :] = zeros_pad
    p0[4:12, PAD : PAD + COLS, :] = wn[0].astype(F32)
    q0[4:12, PAD : PAD + COLS, :] = an[0].astype(F32)
    for j in range(2):
        hb_vel[4, j * 8 : (j + 1) * 8, :] = vel[:, j, :]
    own = pl.ds(pl.multiple_of(xc * 16, 16), 16)
    vg[zh, own, :] = hb_vel[4]

    pl.semaphore_wait(barrier, len(greeted))

    def halo(field, index):
        inner = pl.ds(PAD, COLS)
        a = send(
            field.at[pl.ds(8, 4), inner, :], field.at[pl.ds(0, 4), inner, :],
            s_hal.at[index], r_hal.at[index], (shot, up),
        )
        b = send(
            field.at[pl.ds(4, 4), inner, :], field.at[pl.ds(12, 4), inner, :],
            s_hal.at[index + 1], r_hal.at[index + 1], (shot, down),
        )
        return a, b

    def halo_wait(field, copies):
        for copy in copies:
            copy.wait_recv()

        @pl.when(sub == 0)
        def _():
            field[0:4, PAD : PAD + COLS, :] = jnp.zeros((4, COLS, DEPTH), F32)

        @pl.when(sub == N_SUB - 1)
        def _():
            field[12:16, PAD : PAD + COLS, :] = jnp.zeros((4, COLS, DEPTH), F32)

    v1 = [
        send(hb_vel.at[4], vg.at[zh, own, :], s_v1.at[k - 1], r_v1.at[k - 1], zh_peer(k)) for k in range(1, 4)
    ]
    halo_p0 = halo(p0, 0)
    halo_q0 = halo(q0, 2)
    for copy in v1:
        copy.wait_recv()
    v2 = [
        send(vg.at[:, own, :], vg.at[:, own, :], s_v2.at[k - 1], r_v2.at[k - 1], xc_peer(k)) for k in range(1, 8)
    ]

    def around_sends(buffer, ssem, rsem):
        return [
            send(
                buffer.at[4], buffer.at[(1 - d) * 3 + (1 - e)], ssem.at[n], rsem.at[n], near(d, e)
            )
            for n, (d, e) in enumerate(around)
        ]

    hv = around_sends(hb_vel, s_hv, r_hv)

    cells = rcell[0].astype(F32).astype(BF16)
    pick = (
        lax.broadcasted_iota(jnp.int32, (8, 2), 0) == lax.broadcasted_iota(jnp.int32, (8, 2), 1)
    ).astype(F32).astype(BF16)
    cells_t = dot_t(pick, cells)
    rec_x = cells_t[0:1, :]
    rec_y = cells_t[1:2, :]
    hit_y = (
        lax.broadcasted_iota(jnp.int32, (COLS, 256), 0).astype(F32) == jnp.broadcast_to(rec_y, (COLS, 256))
    ).astype(F32).astype(BF16)
    rows_here = (lax.broadcasted_iota(jnp.int32, (8, 256), 0) + x0).astype(F32)
    hit_x = (rows_here == jnp.broadcast_to(rec_x, (8, 256))).astype(F32)
    trace = jnp.concatenate([hit_x * rtrace[0, 0:1, :], hit_x * rtrace[0, 1:2, :]], axis=0)
    t_hi, t_rest = trace.astype(BF16), trace - trace.astype(BF16).astype(F32)
    t_mid, t_lo = halves(t_rest)
    surf[:, 0:16] = dot_t(hit_y, t_hi) + dot_t(hit_y, t_mid) + dot_t(hit_y, t_lo)

    lane = lax.broadcasted_iota(jnp.int32, (16, HID), 1)
    tile = lane >> 7
    hid_y = (tile >= 12).astype(jnp.int32) + (tile >= 24).astype(jnp.int32) + (tile >= 36).astype(jnp.int32)
    hid_x = tile - 12 * hid_y
    cell_x = hid_x + (x0 - 1)
    cell_y = hid_y + (2 * shot - 1)
    mask[...] = (
        (hid_x < 10) & (cell_x >= 0) & (cell_x < GRID_X) & (cell_y >= 0) & (cell_y < GRID_Y)
    ).astype(F32)
    gs[...] = jnp.where(lax.broadcasted_iota(jnp.int32, (TILES * 8, DEPTH), 0) % 8 == 6, 1.0, 0.0)
    rs[...] = jnp.zeros((TILES * 8, DEPTH), F32)

    z_row = lax.broadcasted_iota(jnp.int32, (COLS, DEPTH), 1)
    y_row = lax.broadcasted_iota(jnp.int32, (COLS, DEPTH), 0)
    source_yz = jnp.where((y_row == scell[0, 1]) & (z_row == scell[0, 2]), 1.0, 0.0)
    rec_mark = z_row == ZREC
    back_w = [None] + [jnp.where(z_row[0:8] >= k, COEFFS[k], 0.0) for k in range(1, 5)]
    fore_w = [None] + [jnp.where(z_row[0:8] < DEPTH - k, COEFFS[k], 0.0) for k in range(1, 5)]

    def tall(w):
        return jnp.broadcast_to(w[0:1], (COLS, DEPTH))

    def lap_row(field, i):
        inner = pl.ds(PAD, COLS)
        center = field[i + 4, inner, :]
        out = (3.0 * COEFFS[0]) * center
        for k in range(1, 5):
            out = out + COEFFS[k] * (
                (field[i + 4 + k, inner, :] + field[i + 4 - k, inner, :])
                + (field[i + 4, pl.ds(PAD + k, COLS), :] + field[i + 4, pl.ds(PAD - k, COLS), :])
            )
            out = out + pltpu.roll(center, k, 1) * tall(back_w[k])
            out = out + pltpu.roll(center, DEPTH - k, 1) * tall(fore_w[k])
        return center, out

    def source(i, step):
        amount = jnp.where(scell[0, 0] == x0 + i, swave[0, step], 0.0)
        return amount * source_yz

    def receivers(i, step):
        column = pltpu.roll(surf[...], (DEPTH + ZREC - step * 8 - i) % DEPTH, 1)
        return jnp.where(rec_mark, column, 0.0)

    for copy in v2:
        copy.wait_recv()
    for z in range(4):
        for i in range(ROWS):
            vfull[i, z * 16 : (z + 1) * 16, :] = vg.at[z][pl.ds(i, 16, stride=8), :]
    halo_wait(p0, halo_p0)

    def forward_0(i, carry):
        center, lap = lap_row(p0, i)
        lap0[i] = lap
        p1[i + 4, pl.ds(PAD, COLS), :] = (
            2.0 * center - wb[0, i].astype(F32) + vfull[i] * lap + source(i, 0)
        )
        return carry

    lax.fori_loop(0, ROWS, forward_0, 0)
    halo_p1 = halo(p1, 4)

    halo_wait(q0, halo_q0)

    def adjoint_0(i, carry):
        center, lap = lap_row(q0, i)
        q1[i + 4, pl.ds(PAD, COLS), :] = (
            2.0 * center - ab[0, i].astype(F32) + vfull[i] * lap + receivers(i, 0)
        )
        return carry

    lax.fori_loop(0, ROWS, adjoint_0, 0)
    halo_q1 = halo(q1, 6)

    ok_shot = {-1: shot > 0, 0: None, 1: shot < N_SHOT - 1}
    ok_sub = {-1: sub > 0, 0: None, 1: sub < N_SUB - 1}

    def channel(buffer, which, centered):
        for d in (-1, 0, 1):
            for e in (-1, 0, 1):
                for j in range(2):
                    block = buffer[(d + 1) * 3 + (e + 1), j * 8 : (j + 1) * 8, :]
                    if centered:
                        block = (block - CENTER_SHIFT) * CENTER_GAIN
                    for ok in (ok_shot[d], ok_sub[e]):
                        if ok is not None:
                            block = block * jnp.where(ok, 1.0, 0.0)
                    row = (2 + 2 * d + j) * WIDE
                    if e == -1:
                        ext[row : row + 2, :] = block[6:8]
                    elif e == 0:
                        ext[row + 2 : row + 10, :] = block
                    else:
                        ext[row + 10 : row + 12, :] = block[0:2]
        value = ext[...]
        for dz in range(3):
            gs[pl.ds(which * 3 + dz, 72, stride=8), :] = shifted(value, dz - 1)

    for copy in hv:
        copy.wait_recv()
    channel(hb_vel, 1, True)

    halo_wait(p1, halo_p1)

    def forward_1(i, carry):
        center, lap = lap_row(p1, i)
        fresh = 2.0 * center - p0[i + 4, pl.ds(PAD, COLS), :] + vfull[i] * lap + source(i, 1)
        nw[0, i] = fresh.astype(BF16)
        imgacc[i] = lap * q1[i + 4, pl.ds(PAD, COLS), :]
        return carry

    lax.fori_loop(0, ROWS, forward_1, 0)

    halo_wait(q1, halo_q1)

    def adjoint_1(i, carry):
        center, lap = lap_row(q1, i)
        fresh = 2.0 * center - q0[i + 4, pl.ds(PAD, COLS), :] + vfull[i] * lap + receivers(i, 1)
        imgacc[i] = imgacc[i] + lap0[i] * fresh
        return carry

    lax.fori_loop(0, ROWS, adjoint_1, 0)
    for z in range(4):
        for i in range(ROWS):
            imgt.at[z][pl.ds(i, 16, stride=8), :] = imgacc[i, z * 16 : (z + 1) * 16, :]

    sends_a = [
        send(
            imgt.at[:, pl.ds(pl.multiple_of(((xc + k) % 8) * 16, 16), 16), :], ra.at[k - 1],
            s_a.at[k - 1], r_a.at[k - 1], xc_peer(k),
        )
        for k in range(1, 8)
    ]
    total = imgt[:, own, :]
    for k in range(1, 8):
        sends_a[k - 1].wait_recv()
        total = total + ra[k - 1]
    acca[...] = total
    sends_b = [
        send(acca.at[(zh + k) % 4], rb.at[k - 1], s_b.at[k - 1], r_b.at[k - 1], zh_peer(k)) for k in range(1, 4)
    ]
    total = acca[zh]
    for k in range(1, 4):
        sends_b[k - 1].wait_recv()
        total = total + rb[k - 1]
    hb_img[4] = total * (1.0 / N_SHOT)
    sends_c = around_sends(hb_img, s_c, r_c)

    w1, k2 = wpack[:, 0:80], wpack[:, 128:208]
    w1_hi, w1_lo = halves(w1)
    k2_hi, k2_lo = halves(k2)
    w1_cat = jnp.concatenate([w1_hi, w1_hi, w1_lo], axis=1)
    k2_cat = jnp.concatenate([k2_hi, k2_hi, k2_lo], axis=1)
    unit = (
        lax.broadcasted_iota(jnp.int32, (80, 80), 0) == lax.broadcasted_iota(jnp.int32, (80, 80), 1)
    ).astype(F32).astype(BF16)
    k2t_hi = dot_t(unit, k2_hi).astype(BF16)
    k2t_lo = dot_t(unit, k2_lo).astype(BF16)
    k2t_cat = jnp.concatenate([k2t_hi, k2t_hi, k2t_lo], axis=1)

    for copy in sends_c:
        copy.wait_recv()
    channel(hb_img, 0, False)

    def spread(source_ref, target_ref):
        for t in range(TILES):
            target_ref[:, t * DEPTH : (t + 1) * DEPTH] = source_ref[t * 8 : (t + 1) * 8, :]

    def stacked(ref, offsets, start):
        parts = [ref[:, start + o * DEPTH : start + o * DEPTH + CHUNK] for o in offsets]
        return jnp.concatenate(parts, axis=0)

    spread(gs, g2)
    for start in range(0, HID, CHUNK):
        here = slice(start, start + CHUNK)
        f_hi, f_lo = halves(stacked(g2, OFFSETS + (0,), start))
        fhi[:, here] = f_hi
        flo[:, here] = f_lo
        pre = dot(w1_cat, jnp.concatenate([f_hi, f_lo, f_hi], axis=0))
        hidden = jnp.tanh(pre) * mask[:, here]
        hid[:, here] = hidden
        h_hi, h_lo = halves(hidden)
        smat[:, here] = dot(k2t_cat, jnp.concatenate([h_hi, h_lo, h_hi], axis=0))

    span = 20 * DEPTH
    turned = smat[0:8, 0:span]
    for n in range(1, 9):
        turned = turned + smat[n * 8 : n * 8 + 8, OFFSETS[n] * DEPTH : OFFSETS[n] * DEPTH + span]
    for t in range(20):
        tt[t * 8 : t * 8 + 8, :] = turned[:, t * DEPTH : (t + 1) * DEPTH]
    bias_sum = jnp.zeros((8, DEPTH), F32)
    for j in range(2):
        update = b2[0]
        for dz in range(3):
            update = update + shifted(tt[pl.ds(j * WIDE * 8 + dz, 8, stride=8), :], dz - 1)
        fresh = hb_vel[4, j * 8 : (j + 1) * 8, :] - update
        nv[:, j, :] = fresh
        slope = tgt[:, j, :] - fresh
        bias_sum = bias_sum + slope
        for dz in range(3):
            rs[pl.ds(((j + 2) * WIDE + 2) * 8 + dz, 8, stride=8), :] = shifted(slope, 1 - dz)

    spread(rs, r2)
    offsets_r = tuple((2 - dy) * WIDE + (2 - dx) for dx in range(3) for dy in range(3)) + (0,)
    grad_1 = jnp.zeros((32, 160), F32)
    grad_2 = jnp.zeros((32, 160), F32)
    for start in range(0, HID, CHUNK):
        here = slice(start, start + CHUNK)
        r_hi, r_lo = halves(stacked(r2, offsets_r, start))
        slope_h = dot(k2_cat, jnp.concatenate([r_hi, r_lo, r_hi], axis=0))
        hidden = hid[:, here]
        h_hi, h_lo = halves(hidden)
        grad_2 = grad_2 + dot_t(jnp.concatenate([h_hi, h_lo], axis=0), jnp.concatenate([r_hi, r_lo], axis=0))
        d_hi, d_lo = halves(slope_h * (1.0 - hidden * hidden) * mask[:, here])
        grad_1 = grad_1 + dot_t(
            jnp.concatenate([d_hi, d_lo], axis=0), jnp.concatenate([fhi[:, here], flo[:, here]], axis=0)
        )

    def joined(grad):
        value = (grad[0:16, 0:80] + grad[0:16, 80:160]) + grad[16:32, 0:80]
        return jnp.concatenate([value, jnp.zeros((16, 48), F32)], axis=1)

    gk1, gk2 = joined(grad_1), joined(grad_2)
    col = lax.broadcasted_iota(jnp.int32, (16, DEPTH), 1)
    row = lax.broadcasted_iota(jnp.int32, (16, DEPTH), 0)
    pack = jnp.where((col < 72) & ((col % 8 < 6) | (col == 38)), gk1, 0.0)
    for n in range(9):
        moved = pltpu.roll(gk2, 72 + 3 * n - 8 * n, 1)
        pack = jnp.where((col >= 72 + 3 * n) & (col < 75 + 3 * n), moved, pack)
    bias = jnp.sum(jnp.sum(bias_sum, axis=0, keepdims=True), axis=1, keepdims=True)
    pack = jnp.where((col == 99) & (row == 0), jnp.broadcast_to(bias, (16, DEPTH)), pack)

    for level, (me, peer) in enumerate(((xc, xc_peer), (zz, z_peer), (yy, y_peer))):
        re[level, me] = pack
        copies = [
            send(
                re.at[level, me], re.at[level, me], s_e.at[level * 7 + k - 1], r_e.at[level * 7 + k - 1], peer(k)
            )
            for k in range(1, 8)
        ]
        for copy in copies:
            copy.wait_recv()
        pack = re[level, 0]
        for n in range(1, 8):
            pack = pack + re[level, n]

    squares = jnp.sum(jnp.sum(pack * pack, axis=0, keepdims=True), axis=1, keepdims=True)
    factor = 1.0 / jnp.sqrt(squares * (1.0 / ENTRIES) + 1e-06)
    moves[...] = pack * factor

    for copy in pending:
        copy.wait_send()


def shards(
    wave_before, wave_now, adjoint_before, adjoint_now, velocity, target_model, source_cell, source_wave,
    receiver_cell, receiver_trace, first_kernel, first_bias, second_kernel, second_bias,
):
    w1 = first_kernel.transpose(0, 2, 3, 1, 4).reshape(16, 9, 6)
    bias = jnp.zeros((16, 9, 1), F32).at[:, 4, 0].set(first_bias)
    w1 = jnp.pad(jnp.concatenate([w1, bias], axis=2), ((0, 0), (0, 0), (0, 1))).reshape(16, 72)
    k2 = jnp.pad(second_kernel.reshape(16, 9, 3), ((0, 0), (0, 0), (0, 5))).reshape(16, 72)
    wpack = jnp.concatenate([jnp.pad(w1, ((0, 0), (0, 56))), jnp.pad(k2, ((0, 0), (0, 56)))], axis=1)

    vmem = pl.BlockSpec(memory_space=pltpu.VMEM)
    smem = pl.BlockSpec(memory_space=pltpu.SMEM)
    dma = pltpu.SemaphoreType.DMA
    field = pltpu.VMEM((16, COLS + 2 * PAD, DEPTH), F32)
    block = pltpu.VMEM((ROWS, COLS, DEPTH), F32)
    scratch = [
        field, field, field, field, block, block, block,
        pltpu.VMEM((4, DEPTH, DEPTH), F32),
        pltpu.VMEM((COLS, DEPTH), F32),
        pltpu.VMEM((4, DEPTH, DEPTH), F32),
        pltpu.VMEM((7, 4, 16, DEPTH), F32),
        pltpu.VMEM((4, 16, DEPTH), F32),
        pltpu.VMEM((3, 16, DEPTH), F32),
        pltpu.VMEM((9, 16, DEPTH), F32),
        pltpu.VMEM((9, 16, DEPTH), F32),
        pltpu.VMEM((72, DEPTH), F32),
        pltpu.VMEM((TILES * 8, DEPTH), F32),
        pltpu.VMEM((8, TILES * DEPTH), F32),
        pltpu.VMEM((TILES * 8, DEPTH), F32),
        pltpu.VMEM((8, TILES * DEPTH), F32),
        pltpu.VMEM((80, HID), BF16),
        pltpu.VMEM((80, HID), BF16),
        pltpu.VMEM((16, HID), F32),
        pltpu.VMEM((80, HID), F32),
        pltpu.VMEM((160, DEPTH), F32),
        pltpu.VMEM((16, HID), F32),
        pltpu.VMEM((3, 8, 16, DEPTH), F32),
    ]
    for count in (8, 3, 7, 8, 7, 3, 8, 21):
        scratch += [dma((count,)), dma((count,))]
    next_wave, new_velocity, moves = pl.pallas_call(
        kernel,
        out_shape=(
            jax.ShapeDtypeStruct(wave_now.shape, BF16),
            jax.ShapeDtypeStruct(velocity.shape, F32),
            jax.ShapeDtypeStruct((16, DEPTH), F32),
        ),
        in_specs=[vmem, vmem, vmem, vmem, vmem, vmem, smem, smem, vmem, vmem, vmem, smem],
        out_specs=(vmem, vmem, vmem),
        scratch_shapes=scratch,
        compiler_params=pltpu.CompilerParams(
            collective_id=0, has_side_effects=True, vmem_limit_bytes=40 * 1024 * 1024
        ),
    )(
        wave_before, wave_now, adjoint_before, adjoint_now, velocity, target_model, source_cell, source_wave,
        receiver_cell, receiver_trace, wpack, second_bias,
    )
    taps = moves[:, 0:72].reshape(16, 3, 3, 8)
    first_move = taps[..., 0:6].reshape(16, 3, 3, 2, 3).transpose(0, 3, 1, 2, 4)
    return (
        next_wave,
        new_velocity,
        first_move,
        moves[:, 38],
        moves[:, 72:99].reshape(1, 16, 3, 3, 3),
        moves[0, 99:100],
    )


def solution(mesh):
    return jax.shard_map(
        shards,
        mesh=mesh,
        in_specs=(
            P("shot", "sub", None, None),
            P("shot", "sub", None, None),
            P("shot", "sub", None, None),
            P("shot", "sub", None, None),
            P("sub", "shot", None),
            P("sub", "shot", None),
            P("shot", None),
            P("shot", None),
            P("shot", None, None),
            P("shot", None, None),
            P(),
            P(),
            P(),
            P(),
        ),
        out_specs=(P("shot", "sub", None, None), P("sub", "shot", None), P(), P(), P(), P()),
        check_vma=False,
    )
```

```python
import functools

import jax
import jax.numpy as jnp
from jax import lax
from jax.experimental import pallas as pl
from jax.experimental.pallas import tpu as pltpu
from jax.sharding import PartitionSpec as P

F32 = jnp.float32
BF16 = jnp.bfloat16
MESH = pl.DeviceIdType.MESH

ZREC = 2
COEFFS = (-205.0 / 72.0, 8.0 / 5.0, -1.0 / 5.0, 8.0 / 315.0, -1.0 / 560.0)
CENTER_SHIFT = 0.125
CENTER_GAIN = 16.0
ENTRIES = 1313

ROWS = 8
COLS = 64
DEPTH = 128
PAD = 8
N_SHOT, N_SUB = 32, 16
GRID_X, GRID_Y = 128, 64

TILES = 80
WIDE = 12
HID = 48 * DEPTH
CHUNK = 8 * DEPTH
OFFSETS = tuple(dy * WIDE + dx for dx in range(3) for dy in range(3))
BLOCKS = 10


def dot(a, b):
    return jnp.dot(a, b, preferred_element_type=F32)


def dot_t(a, b):
    return lax.dot_general(a, b, (((1,), (1,)), ((), ())), preferred_element_type=F32)


def halves(x):
    high = x.astype(BF16)
    return high, (x - high.astype(F32)).astype(BF16)


def shifted(x, dz):
    if dz == 0:
        return x
    z = lax.broadcasted_iota(jnp.int32, x.shape, 1)
    if dz > 0:
        return jnp.where(z < DEPTH - dz, pltpu.roll(x, DEPTH - dz, 1), 0.0)
    return jnp.where(z >= -dz, pltpu.roll(x, -dz, 1), 0.0)


def kernel(
    wb_in, wn_in, ab_in, an_in, vel_in, tgt_in, scell_in, swave_in, rcell_in, rtrace_in, w1_in, b1_in, k2_in, b2_in,
    nw, nv, moves,
    wb, wn, ab, an, vel, tgt, scell, swave, rcell, rtrace, w1_own, b1, k2_own, b2,
    p0, q0, p1, q1, lap0, lapq, imgacc, vfull, vg, surf, imgt, ra, acca, rb, hb_img, hb_vel,
    ext, gs, g2, rs, r2, fhi, flo, hid, smat, tt, mask, re, wt, kt,
    s_in, s_hal, r_hal, s_v1, r_v1, s_v2, r_v2, s_hv, r_hv, s_a, r_a, s_b, r_b, s_c, r_c, s_e, r_e,
):
    shot = lax.axis_index("shot")
    sub = lax.axis_index("sub")
    zh, xc = shot // 8, shot % 8
    zlo, yy = sub // 8, sub % 8
    zz = zh * 2 + zlo
    x0 = sub * ROWS
    up, down = (sub + 1) % N_SUB, (sub + N_SUB - 1) % N_SUB

    def xc_peer(k):
        return (zh * 8 + (xc + k) % 8, sub)

    def zh_peer(k):
        return (((zh + k) % 4) * 8 + xc, sub)

    def z_peer(k):
        z = (zz + k) % 8
        return ((z // 2) * 8 + xc, (z % 2) * 8 + yy)

    def y_peer(k):
        return (shot, zlo * 8 + (yy + k) % 8)

    def near(d, e):
        return ((shot + d + N_SHOT) % N_SHOT, (sub + e + N_SUB) % N_SUB)

    around = [(d, e) for d in (-1, 0, 1) for e in (-1, 0, 1) if (d, e) != (0, 0)]
    greeted = (
        [near(d, e) for d, e in around]
        + [xc_peer(k) for k in range(1, 8)]
        + [zh_peer(k) for k in range(1, 4)]
        + [z_peer(k) for k in range(1, 8)]
        + [y_peer(k) for k in range(1, 8)]
    )
    barrier = pltpu.get_barrier_semaphore()
    for device in greeted:
        pl.semaphore_signal(barrier, inc=1, device_id=device, device_id_type=MESH)

    loads = [
        pltpu.make_async_copy(outer, inner, s_in.at[n])
        for n, (outer, inner) in enumerate((
            (wn_in, wn), (an_in, an), (vel_in, vel), (wb_in, wb), (ab_in, ab), (rcell_in, rcell),
            (rtrace_in, rtrace), (scell_in, scell), (swave_in, swave), (tgt_in, tgt), (w1_in, w1_own),
            (b1_in, b1), (k2_in, k2_own), (b2_in, b2),
        ))
    ]
    for copy in loads:
        copy.start()

    pending = []

    def settle(keep=0):
        for copy in pending[: len(pending) - keep]:
            copy.wait_send()
        del pending[: len(pending) - keep]

    def send(src, dst, ssem, rsem, device):
        copy = pltpu.make_async_remote_copy(
            src_ref=src, dst_ref=dst, send_sem=ssem, recv_sem=rsem, device_id=device, device_id_type=MESH
        )
        copy.start()
        pending.append(copy)
        return copy

    zeros_pad = jnp.zeros((16, PAD, DEPTH), F32)
    for field in (p0, q0, p1, q1):
        field[:, 0:PAD, :] = zeros_pad
        field[:, PAD + COLS :, :] = zeros_pad
    loads[0].wait()
    p0[4:12, PAD : PAD + COLS, :] = wn[0].astype(F32)
    loads[1].wait()
    q0[4:12, PAD : PAD + COLS, :] = an[0].astype(F32)
    loads[2].wait()
    for j in range(2):
        hb_vel[4, j * 8 : (j + 1) * 8, :] = vel[:, j, :]
    own = pl.ds(pl.multiple_of(xc * 16, 16), 16)
    vg[0, own, :] = hb_vel[4]

    pl.semaphore_wait(barrier, len(greeted))

    every = pl.ds(PAD, COLS)

    def halo(field, index, columns=every):
        return [
            send(
                field.at[pl.ds(8, 4), columns, :], field.at[pl.ds(0, 4), columns, :],
                s_hal.at[index], r_hal.at[index], (shot, up),
            ),
            send(
                field.at[pl.ds(4, 4), columns, :], field.at[pl.ds(12, 4), columns, :],
                s_hal.at[index + 1], r_hal.at[index + 1], (shot, down),
            ),
        ]

    def halo_wait(field, copies):
        for copy in copies:
            copy.wait_recv()

        @pl.when(sub == 0)
        def _():
            field[0:4, PAD : PAD + COLS, :] = jnp.zeros((4, COLS, DEPTH), F32)

        @pl.when(sub == N_SUB - 1)
        def _():
            field[12:16, PAD : PAD + COLS, :] = jnp.zeros((4, COLS, DEPTH), F32)

    behind = (0, 1, 3, 2)
    v1 = [
        send(hb_vel.at[4], vg.at[slot, own, :], s_v1.at[slot - 1], r_v1.at[slot - 1], zh_peer(behind[slot]))
        for slot in (3, 1, 2)
    ]

    def around_sends(buffer, ssem, rsem):
        return [
            send(
                buffer.at[4], buffer.at[(1 - d) * 3 + (1 - e)], ssem.at[n], rsem.at[n], near(d, e)
            )
            for n, (d, e) in enumerate(around)
        ]

    for copy in loads[3:9]:
        copy.wait()
    cells = rcell[0].astype(F32)
    hit_y = (
        lax.broadcasted_iota(jnp.int32, (COLS, 256), 0).astype(F32) == jnp.broadcast_to(cells[1:2], (COLS, 256))
    ).astype(F32).astype(BF16)
    rows_here = (lax.broadcasted_iota(jnp.int32, (8, 256), 0) + x0).astype(F32)
    hit_x = (rows_here == jnp.broadcast_to(cells[0:1], (8, 256))).astype(F32)
    trace = jnp.concatenate([hit_x * rtrace[0, 0:1, :], hit_x * rtrace[0, 1:2, :]], axis=0)
    t_hi, t_rest = trace.astype(BF16), trace - trace.astype(BF16).astype(F32)
    t_mid, t_lo = halves(t_rest)
    surf[:, 0:16] = dot_t(hit_y, t_hi) + dot_t(hit_y, t_mid) + dot_t(hit_y, t_lo)

    z_row = lax.broadcasted_iota(jnp.int32, (COLS, DEPTH), 1)
    y_row = lax.broadcasted_iota(jnp.int32, (COLS, DEPTH), 0)
    source_cell = [jnp.broadcast_to(scell[0:1, n : n + 1], (COLS, DEPTH)) for n in range(3)]
    source_yz = (y_row == source_cell[1]) & (z_row == source_cell[2])
    source_amount = [
        jnp.where(source_yz, jnp.broadcast_to(swave[0:1, n : n + 1], (COLS, DEPTH)), 0.0) for n in range(2)
    ]
    rec_mark = z_row == ZREC
    back_w = [None] + [jnp.where(z_row[0:8] >= k, COEFFS[k], 0.0) for k in range(1, 5)]
    fore_w = [None] + [jnp.where(z_row[0:8] < DEPTH - k, COEFFS[k], 0.0) for k in range(1, 5)]

    def tall(w):
        return jnp.broadcast_to(w[0:1], (COLS, DEPTH))

    def lap_row(field, i):
        center = field[i + 4, every, :]
        out = (3.0 * COEFFS[0]) * center
        for k in range(1, 5):
            out = out + COEFFS[k] * (
                (field[i + 4 + k, every, :] + field[i + 4 - k, every, :])
                + (field[i + 4, pl.ds(PAD + k, COLS), :] + field[i + 4, pl.ds(PAD - k, COLS), :])
            )
            out = out + pltpu.roll(center, k, 1) * tall(back_w[k])
            out = out + pltpu.roll(center, DEPTH - k, 1) * tall(fore_w[k])
        return center, out

    def source(i, step):
        return jnp.where(source_cell[0] == x0 + i, source_amount[step], 0.0)

    def receivers(i, step):
        column = pltpu.roll(surf[...], (DEPTH + ZREC - step * 8 - i) % DEPTH, 1)
        return jnp.where(rec_mark, column, 0.0)

    for copy in v1:
        copy.wait_recv()
    v2 = [
        send(vg.at[:, own, :], vg.at[:, own, :], s_v2.at[k - 1], r_v2.at[k - 1], xc_peer(k)) for k in range(1, 8)
    ]

    halo_p0 = halo(p0, 0)
    halo_q0 = halo(q0, 2)
    halo_wait(p0, halo_p0)

    def forward_0(i, carry):
        center, lap = lap_row(p0, i)
        lap0[i] = lap
        p1[i + 4, every, :] = 2.0 * center - wb[0, i].astype(F32) + source(i, 0)
        return carry

    lax.fori_loop(0, ROWS, forward_0, 0)

    def adjoint_0(i, carry):
        center, lap = lap_row(q0, i)
        lapq[i] = lap
        q1[i + 4, every, :] = 2.0 * center - ab[0, i].astype(F32) + receivers(i, 0)
        return carry

    halo_wait(q0, halo_q0)
    lax.fori_loop(0, ROWS, adjoint_0, 0)

    for copy in v2:
        copy.wait_recv()
    for slot in range(4):
        columns = pl.ds(pl.multiple_of(((zh + 4 - behind[slot]) % 4) * 16, 16), 16)
        for i in range(ROWS):
            vfull[i, columns, :] = vg.at[slot][pl.ds(i, 16, stride=8), :]
    p1[4:12, every, :] = p1[4:12, every, :] + vfull[...] * lap0[...]
    halo_p1 = halo(p1, 4)
    q1[4:12, every, :] = q1[4:12, every, :] + vfull[...] * lapq[...]
    halo_q1 = halo(q1, 6)
    hv = around_sends(hb_vel, s_hv, r_hv)

    halo_wait(p1, halo_p1)

    def forward_1(i, carry):
        center, lap = lap_row(p1, i)
        fresh = 2.0 * center - p0[i + 4, every, :] + vfull[i] * lap + source(i, 1)
        nw[0, i] = fresh.astype(BF16)
        imgacc[i] = lap * q1[i + 4, every, :]
        return carry

    lax.fori_loop(0, ROWS, forward_1, 0)

    halo_wait(q1, halo_q1)

    def adjoint_1(i, carry):
        center, lap = lap_row(q1, i)
        fresh = 2.0 * center - q0[i + 4, every, :] + vfull[i] * lap + receivers(i, 1)
        imgacc[i] = imgacc[i] + lap0[i] * fresh
        return carry

    lax.fori_loop(0, ROWS, adjoint_1, 0)
    for z in range(4):
        for i in range(ROWS):
            imgt.at[z][pl.ds(i, 16, stride=8), :] = imgacc[i, z * 16 : (z + 1) * 16, :]

    sends_a = [
        send(
            imgt.at[:, pl.ds(pl.multiple_of(((xc + k) % 8) * 16, 16), 16), :], ra.at[k - 1],
            s_a.at[k - 1], r_a.at[k - 1], xc_peer(k),
        )
        for k in range(1, 8)
    ]
    settle(7)

    for copy in loads[9:]:
        copy.wait()
    lane = lax.broadcasted_iota(jnp.int32, (16, HID), 1)
    tile = lane >> 7
    hid_y = (tile >= 12).astype(jnp.int32) + (tile >= 24).astype(jnp.int32) + (tile >= 36).astype(jnp.int32)
    hid_x = tile - 12 * hid_y
    cell_x = hid_x + (x0 - 1)
    cell_y = hid_y + (2 * shot - 1)
    mask[...] = (
        (hid_x < 10) & (cell_x >= 0) & (cell_x < GRID_X) & (cell_y >= 0) & (cell_y < GRID_Y)
    ).astype(F32)
    gs[...] = jnp.where(lax.broadcasted_iota(jnp.int32, (TILES * 8, DEPTH), 0) % 8 == 6, 1.0, 0.0)
    rs[...] = jnp.zeros((TILES * 8, DEPTH), F32)
    ok_shot = {-1: shot > 0, 0: None, 1: shot < N_SHOT - 1}
    ok_sub = {-1: sub > 0, 0: None, 1: sub < N_SUB - 1}

    def channel(buffer, which, centered):
        for d in (-1, 0, 1):
            for e in (-1, 0, 1):
                for j in range(2):
                    block = buffer[(d + 1) * 3 + (e + 1), j * 8 : (j + 1) * 8, :]
                    if centered:
                        block = (block - CENTER_SHIFT) * CENTER_GAIN
                    for ok in (ok_shot[d], ok_sub[e]):
                        if ok is not None:
                            block = block * jnp.where(ok, 1.0, 0.0)
                    row = (2 + 2 * d + j) * WIDE
                    if e == -1:
                        ext[row : row + 2, :] = block[6:8]
                    elif e == 0:
                        ext[row + 2 : row + 10, :] = block
                    else:
                        ext[row + 10 : row + 12, :] = block[0:2]
        value = ext[...]
        for dz in range(3):
            gs[pl.ds(which * 3 + dz, 72, stride=8), :] = shifted(value, dz - 1)

    for copy in hv:
        copy.wait_recv()
    channel(hb_vel, 1, True)

    wt[...] = jnp.zeros((80, DEPTH), F32)
    kt[...] = jnp.zeros((80, DEPTH), F32)
    for n in range(9):
        for i in range(2):
            wt[n * 8 + i * 3 : n * 8 + i * 3 + 3, 0:16] = w1_own[n // 3, n % 3, :, i, :]
        kt[n * 8 : n * 8 + 3, 0:16] = k2_own[n // 3, n % 3, :, 0, :]
    wt[38:39, 0:16] = b1[...]
    w1_hi, w1_lo = halves(wt[:, 0:16])
    k2_hi, k2_lo = halves(kt[:, 0:16])
    unit = (
        lax.broadcasted_iota(jnp.int32, (16, 16), 0) == lax.broadcasted_iota(jnp.int32, (16, 16), 1)
    ).astype(F32).astype(BF16)

    def turn(x):
        return dot_t(unit, x).astype(BF16)

    w1_cat = jnp.concatenate([turn(w1_hi), turn(w1_hi), turn(w1_lo)], axis=1)
    k2_cat = jnp.concatenate([turn(k2_hi), turn(k2_hi), turn(k2_lo)], axis=1)
    k2t_cat = jnp.concatenate([k2_hi, k2_hi, k2_lo], axis=1)

    total = imgt[:, own, :]
    for k in range(1, 8):
        sends_a[k - 1].wait_recv()
        total = total + ra[k - 1]
    acca[...] = total
    sends_b = [
        send(acca.at[(zh + k) % 4], rb.at[k - 1], s_b.at[k - 1], r_b.at[k - 1], zh_peer(k)) for k in range(1, 4)
    ]
    settle(3)
    total = acca[zh]
    for k in range(1, 4):
        sends_b[k - 1].wait_recv()
        total = total + rb[k - 1]
    hb_img[4] = total * (1.0 / N_SHOT)
    sends_c = around_sends(hb_img, s_c, r_c)

    settle(8)
    for copy in sends_c:
        copy.wait_recv()
    channel(hb_img, 0, False)

    def spread(source_ref, target_ref):
        for t in range(TILES):
            target_ref[:, t * DEPTH : (t + 1) * DEPTH] = source_ref[t * 8 : (t + 1) * 8, :]

    def stacked(ref, offsets, start):
        parts = [ref[:, start + o * DEPTH : start + o * DEPTH + CHUNK] for o in offsets]
        return jnp.concatenate(parts, axis=0)

    spread(gs, g2)
    for start in range(0, HID, CHUNK):
        here = slice(start, start + CHUNK)
        f_hi, f_lo = halves(stacked(g2, OFFSETS + (0,), start))
        fhi[:, here] = f_hi
        flo[:, here] = f_lo
        pre = dot(w1_cat, jnp.concatenate([f_hi, f_lo, f_hi], axis=0))
        hidden = jnp.tanh(pre) * mask[:, here]
        hid[:, here] = hidden
        h_hi, h_lo = halves(hidden)
        smat[:, here] = dot(k2t_cat, jnp.concatenate([h_hi, h_lo, h_hi], axis=0))

    span = 20 * DEPTH
    turned = smat[0:8, 0:span]
    for n in range(1, 9):
        turned = turned + smat[n * 8 : n * 8 + 8, OFFSETS[n] * DEPTH : OFFSETS[n] * DEPTH + span]
    for t in range(20):
        tt[t * 8 : t * 8 + 8, :] = turned[:, t * DEPTH : (t + 1) * DEPTH]
    bias_sum = jnp.zeros((8, DEPTH), F32)
    for j in range(2):
        update = b2[0]
        for dz in range(3):
            update = update + shifted(tt[pl.ds(j * WIDE * 8 + dz, 8, stride=8), :], dz - 1)
        fresh = hb_vel[4, j * 8 : (j + 1) * 8, :] - update
        nv[:, j, :] = fresh
        slope = tgt[:, j, :] - fresh
        bias_sum = bias_sum + slope
        for dz in range(3):
            rs[pl.ds(((j + 2) * WIDE + 2) * 8 + dz, 8, stride=8), :] = shifted(slope, 1 - dz)

    spread(rs, r2)
    offsets_r = tuple((2 - dy) * WIDE + (2 - dx) for dx in range(3) for dy in range(3)) + (0,)
    grad_1 = jnp.zeros((32, 160), F32)
    grad_2 = jnp.zeros((32, 160), F32)
    for start in range(0, HID, CHUNK):
        here = slice(start, start + CHUNK)
        r_hi, r_lo = halves(stacked(r2, offsets_r, start))
        slope_h = dot(k2_cat, jnp.concatenate([r_hi, r_lo, r_hi], axis=0))
        hidden = hid[:, here]
        h_hi, h_lo = halves(hidden)
        grad_2 = grad_2 + dot_t(jnp.concatenate([h_hi, h_lo], axis=0), jnp.concatenate([r_hi, r_lo], axis=0))
        d_hi, d_lo = halves(slope_h * (1.0 - hidden * hidden) * mask[:, here])
        grad_1 = grad_1 + dot_t(
            jnp.concatenate([d_hi, d_lo], axis=0), jnp.concatenate([fhi[:, here], flo[:, here]], axis=0)
        )

    def joined(grad):
        value = (grad[0:16, 0:80] + grad[0:16, 80:160]) + grad[16:32, 0:80]
        return jnp.concatenate([value, jnp.zeros((16, 48), F32)], axis=1)

    gk1, gk2 = joined(grad_1), joined(grad_2)
    col = lax.broadcasted_iota(jnp.int32, (16, DEPTH), 1)
    row = lax.broadcasted_iota(jnp.int32, (16, DEPTH), 0)
    pack = jnp.where((col < 72) & ((col % 8 < 6) | (col == 38)), gk1, 0.0)
    for n in range(9):
        moved = pltpu.roll(gk2, 72 + 3 * n - 8 * n, 1)
        pack = jnp.where((col >= 72 + 3 * n) & (col < 75 + 3 * n), moved, pack)
    bias = jnp.sum(jnp.sum(bias_sum, axis=0, keepdims=True), axis=1, keepdims=True)
    pack = jnp.where((col == 99) & (row == 0), jnp.broadcast_to(bias, (16, DEPTH)), pack)

    for level, (me, peer) in enumerate(((xc, xc_peer), (zz, z_peer), (yy, y_peer))):
        re[level, me] = pack
        copies = [
            send(
                re.at[level, me], re.at[level, me], s_e.at[level * 7 + k - 1], r_e.at[level * 7 + k - 1], peer(k)
            )
            for k in range(1, 8)
        ]
        settle(7)
        for copy in copies:
            copy.wait_recv()
        pack = re[level, 0]
        for n in range(1, 8):
            pack = pack + re[level, n]

    squares = jnp.sum(jnp.sum(pack * pack, axis=0, keepdims=True), axis=1, keepdims=True)
    factor = 1.0 / jnp.sqrt(squares * (1.0 / ENTRIES) + 1e-06)
    moves[...] = pack * factor

    settle()


def writer(nw, nv, moves, nw_out, nv_out, w1_out, b1_out, k2_out, b2_out, nw_own, nv_own, pack, w1_own, k2_own, sem):
    def copy(source, target, n):
        move = pltpu.make_async_copy(source, target, sem.at[n])
        move.start()
        return move

    loads = [copy(moves, pack, 0), copy(nw, nw_own, 1), copy(nv, nv_own, 2)]
    loads[0].wait()
    turned = jnp.transpose(pack[...])
    for n in range(9):
        for i in range(2):
            w1_own[n // 3, n % 3, :, i, :] = turned[n * 8 + i * 3 : n * 8 + i * 3 + 3]
        k2_own[n // 3, n % 3, :, 0, :] = turned[72 + 3 * n : 75 + 3 * n]
    b1_out[...] = turned[38:39]
    b2_out[...] = pack[0:1, 99:100]
    stores = [copy(w1_own, w1_out, 3), copy(k2_own, k2_out, 4)]
    loads[1].wait()
    stores.append(copy(nw_own, nw_out, 5))
    loads[2].wait()
    stores.append(copy(nv_own, nv_out, 6))
    for move in stores:
        move.wait()


def shards(
    wave_before, wave_now, adjoint_before, adjoint_now, velocity, target_model, source_cell, source_wave,
    receiver_cell, receiver_trace, first_kernel, first_bias, second_kernel, second_bias,
):
    operands = (
        wave_before, wave_now, adjoint_before, adjoint_now, velocity, target_model, source_cell, source_wave,
        receiver_cell.transpose(0, 2, 1), receiver_trace, first_kernel.transpose(2, 3, 4, 1, 0),
        first_bias.reshape(1, 16), second_kernel.transpose(2, 3, 4, 0, 1), second_bias,
    )
    vmem = pl.BlockSpec(memory_space=pltpu.VMEM)
    hbm = pl.BlockSpec(memory_space=pltpu.HBM)
    dma = pltpu.SemaphoreType.DMA
    field = pltpu.VMEM((16, COLS + 2 * PAD, DEPTH), F32)
    block = pltpu.VMEM((ROWS, COLS, DEPTH), F32)
    scratch = [pltpu.VMEM(x.shape, x.dtype) for x in operands[:-1]] + [pltpu.SMEM((1,), F32)] + [
        field, field, field, field, block, block, block, block,
        pltpu.VMEM((4, DEPTH, DEPTH), F32),
        pltpu.VMEM((COLS, DEPTH), F32),
        pltpu.VMEM((4, DEPTH, DEPTH), F32),
        pltpu.VMEM((7, 4, 16, DEPTH), F32),
        pltpu.VMEM((4, 16, DEPTH), F32),
        pltpu.VMEM((3, 16, DEPTH), F32),
        pltpu.VMEM((9, 16, DEPTH), F32),
        pltpu.VMEM((9, 16, DEPTH), F32),
        pltpu.VMEM((72, DEPTH), F32),
        pltpu.VMEM((TILES * 8, DEPTH), F32),
        pltpu.VMEM((8, TILES * DEPTH), F32),
        pltpu.VMEM((TILES * 8, DEPTH), F32),
        pltpu.VMEM((8, TILES * DEPTH), F32),
        pltpu.VMEM((80, HID), BF16),
        pltpu.VMEM((80, HID), BF16),
        pltpu.VMEM((16, HID), F32),
        pltpu.VMEM((80, HID), F32),
        pltpu.VMEM((160, DEPTH), F32),
        pltpu.VMEM((16, HID), F32),
        pltpu.VMEM((3, 8, 16, DEPTH), F32),
        pltpu.VMEM((80, DEPTH), F32),
        pltpu.VMEM((80, DEPTH), F32),
        dma((len(operands),)),
    ]
    for count in (8, 3, 7, 8, 7, 3, 8, 21):
        scratch += [dma((count,)), dma((count,))]
    next_wave, new_velocity, moves = pl.pallas_call(
        kernel,
        out_shape=(
            jax.ShapeDtypeStruct(wave_now.shape, BF16),
            jax.ShapeDtypeStruct(velocity.shape, F32),
            jax.ShapeDtypeStruct((16, DEPTH), F32),
        ),
        in_specs=[hbm] * len(operands),
        out_specs=(vmem, vmem, vmem),
        scratch_shapes=scratch,
        compiler_params=pltpu.CompilerParams(
            collective_id=0, has_side_effects=True, vmem_limit_bytes=60 * 1024 * 1024
        ),
    )(*operands)
    outs = (
        jax.ShapeDtypeStruct(wave_now.shape, BF16),
        jax.ShapeDtypeStruct(velocity.shape, F32),
        jax.ShapeDtypeStruct((3, 3, 3, 2, 16), F32),
        jax.ShapeDtypeStruct((1, 16), F32),
        jax.ShapeDtypeStruct((3, 3, 3, 1, 16), F32),
        jax.ShapeDtypeStruct((1, 1), F32),
    )
    next_wave, new_velocity, w1, b1, k2, b2 = pl.pallas_call(
        writer,
        out_shape=outs,
        in_specs=[hbm, hbm, hbm],
        out_specs=(hbm, hbm, hbm, vmem, hbm, vmem),
        scratch_shapes=[
            pltpu.VMEM(outs[0].shape, BF16), pltpu.VMEM(outs[1].shape, F32), pltpu.VMEM((16, DEPTH), F32),
            pltpu.VMEM(outs[2].shape, F32), pltpu.VMEM(outs[4].shape, F32), dma((7,)),
        ],
    )(next_wave, new_velocity, moves)
    return (
        next_wave,
        new_velocity,
        w1.transpose(4, 3, 0, 1, 2),
        b1.reshape(16),
        k2.transpose(3, 4, 0, 1, 2),
        b2.reshape(1),
    )


def solution(mesh):
    return jax.shard_map(
        shards,
        mesh=mesh,
        in_specs=(
            P("shot", "sub", None, None),
            P("shot", "sub", None, None),
            P("shot", "sub", None, None),
            P("shot", "sub", None, None),
            P("sub", "shot", None),
            P("sub", "shot", None),
            P("shot", None),
            P("shot", None),
            P("shot", None, None),
            P("shot", None, None),
            P(),
            P(),
            P(),
            P(),
        ),
        out_specs=(P("shot", "sub", None, None), P("sub", "shot", None), P(), P(), P(), P()),
        check_vma=False,
    )
```

```python
import functools

import jax
import jax.numpy as jnp
from jax import lax
from jax.experimental import pallas as pl
from jax.experimental.pallas import tpu as pltpu
from jax.sharding import PartitionSpec as P

F32 = jnp.float32
BF16 = jnp.bfloat16
MESH = pl.DeviceIdType.MESH

ZREC = 2
COEFFS = (-205.0 / 72.0, 8.0 / 5.0, -1.0 / 5.0, 8.0 / 315.0, -1.0 / 560.0)
CENTER_SHIFT = 0.125
CENTER_GAIN = 16.0
ENTRIES = 1313

ROWS = 8
COLS = 64
DEPTH = 128
PAD = 8
N_SHOT, N_SUB = 32, 16
GRID_X, GRID_Y = 128, 64

TILES = 80
WIDE = 12
HID = 48 * DEPTH
CHUNK = 8 * DEPTH
OFFSETS = tuple(dy * WIDE + dx for dx in range(3) for dy in range(3))
BLOCKS = 10


def dot(a, b):
    return jnp.dot(a, b, preferred_element_type=F32)


def dot_t(a, b):
    return lax.dot_general(a, b, (((1,), (1,)), ((), ())), preferred_element_type=F32)


def halves(x):
    high = x.astype(BF16)
    return high, (x - high.astype(F32)).astype(BF16)


def shifted(x, dz):
    if dz == 0:
        return x
    z = lax.broadcasted_iota(jnp.int32, x.shape, 1)
    if dz > 0:
        return jnp.where(z < DEPTH - dz, pltpu.roll(x, DEPTH - dz, 1), 0.0)
    return jnp.where(z >= -dz, pltpu.roll(x, -dz, 1), 0.0)


def kernel(
    wb_in, wn_in, ab_in, an_in, vel_in, tgt_in, scell_in, swave_in, rcell_in, rtrace_in, w1_in, b1_in, k2_in, b2_in,
    nw, nv, moves,
    wb, wn, ab, an, vel, tgt, scell, swave, rcell, rtrace, w1_own, b1, k2_own, b2,
    p0, q0, p1, q1, lap0, lapq, imgacc, vfull, vg, surf, imgt, ra, acca, edge, whole, sides, hb_vel,
    ext, gs, g2, rs, r2, fhi, flo, hid, smat, tt, mask, re, wt, kt,
    s_in, s_hal, r_hal, s_v1, r_v1, s_v2, r_v2, s_hv, r_hv, s_a, r_a, s_b, r_b, s_e, r_e,
):
    shot = lax.axis_index("shot")
    sub = lax.axis_index("sub")
    zh, xc = lax.div(shot, 8), lax.rem(shot, 8)
    zlo, yy = lax.div(sub, 8), lax.rem(sub, 8)
    zz = zh * 2 + zlo
    x0 = sub * ROWS
    up, down = lax.rem(sub + 1, N_SUB), lax.rem(sub + (N_SUB - 1), N_SUB)

    def xc_peer(k):
        return (zh * 8 + lax.rem(xc + k, 8), sub)

    def zh_peer(k):
        return (lax.rem(zh + k, 4) * 8 + xc, sub)

    def z_peer(k):
        z = lax.rem(zz + k, 8)
        return (lax.div(z, 2) * 8 + xc, lax.rem(z, 2) * 8 + yy)

    def y_peer(k):
        return (shot, zlo * 8 + lax.rem(yy + k, 8))

    def near(d, e):
        return (lax.rem(shot + (d + N_SHOT), N_SHOT), lax.rem(sub + (e + N_SUB), N_SUB))

    around = [(d, e) for d in (-1, 0, 1) for e in (-1, 0, 1) if (d, e) != (0, 0)]
    def user(k, d, e):
        owner = lax.rem(zh + k, 4) * 8 + xc
        return (lax.rem(owner + (d + N_SHOT), N_SHOT), lax.rem(sub + (e + N_SUB), N_SUB))

    users = [(k, d, e) for k in (2, 1, 3, 0) for d in (1, -1, 0) for e in (1, -1, 0) if (k, d, e) != (0, 0, 0)]
    twin = (shot, lax.rem(sub + 8, N_SUB))
    greeted = [xc_peer(k) for k in range(1, 8)] + [zh_peer(k) for k in range(1, 4)] + [twin]
    greeted += [near(d, e) for d, e in around]
    barrier = pltpu.get_barrier_semaphore()
    for device in greeted:
        pl.semaphore_signal(barrier, inc=1, device_id=device, device_id_type=MESH)

    loads = [
        pltpu.make_async_copy(outer, inner, s_in.at[n])
        for n, (outer, inner) in enumerate((
            (vel_in, vel), (wn_in, wn), (an_in, an), (wb_in, wb), (ab_in, ab), (rcell_in, rcell),
            (rtrace_in, rtrace), (scell_in, scell), (swave_in, swave), (tgt_in, tgt), (w1_in, w1_own),
            (b1_in, b1), (k2_in, k2_own), (b2_in, b2),
        ))
    ]
    for copy in loads:
        copy.start()

    pending = []

    def settle(keep=0):
        for copy in pending[: len(pending) - keep]:
            copy.wait_send()
        del pending[: len(pending) - keep]

    def send(src, dst, ssem, rsem, device):
        copy = pltpu.make_async_remote_copy(
            src_ref=src, dst_ref=dst, send_sem=ssem, recv_sem=rsem, device_id=device, device_id_type=MESH
        )
        copy.start()
        pending.append(copy)
        return copy

    loads[0].wait()
    for j in range(2):
        hb_vel[4, j * 8 : (j + 1) * 8, :] = vel[:, j, :]
    own = pl.ds(pl.multiple_of(xc * 16, 16), 16)

    pl.semaphore_wait(barrier, len(greeted))

    every = pl.ds(PAD, COLS)

    def halo(field, index, columns=every):
        return [
            send(
                field.at[pl.ds(8, 4), columns, :], field.at[pl.ds(0, 4), columns, :],
                s_hal.at[index], r_hal.at[index], (shot, up),
            ),
            send(
                field.at[pl.ds(4, 4), columns, :], field.at[pl.ds(12, 4), columns, :],
                s_hal.at[index + 1], r_hal.at[index + 1], (shot, down),
            ),
        ]

    def halo_wait(field, copies):
        for copy in copies:
            copy.wait_recv()

        @pl.when(sub == 0)
        def _():
            field[0:4, PAD : PAD + COLS, :] = jnp.zeros((4, COLS, DEPTH), F32)

        @pl.when(sub == N_SUB - 1)
        def _():
            field[12:16, PAD : PAD + COLS, :] = jnp.zeros((4, COLS, DEPTH), F32)

    behind = (0, 1, 3, 2)
    v1 = [
        send(hb_vel.at[4], vg.at[slot, own, :], s_v1.at[slot - 1], r_v1.at[slot - 1], zh_peer(behind[slot]))
        for slot in (3, 1, 2)
    ]

    vg[0, own, :] = hb_vel[4]

    loads[1].wait()
    p0[4:12, every, :] = wn[0].astype(F32)
    halo_p0 = halo(p0, 0)
    loads[2].wait()
    q0[4:12, every, :] = an[0].astype(F32)
    zeros_pad = jnp.zeros((16, PAD, DEPTH), F32)
    for field in (p0, q0, p1, q1):
        field[:, 0:PAD, :] = zeros_pad
        field[:, PAD + COLS :, :] = zeros_pad

    def around_sends(buffer, ssem, rsem):
        return [
            send(
                buffer.at[4], buffer.at[(1 - d) * 3 + (1 - e)], ssem.at[n], rsem.at[n], near(d, e)
            )
            for n, (d, e) in enumerate(around)
        ]

    for copy in loads[3:9]:
        copy.wait()
    cells = rcell[0].astype(F32)
    hit_y = (
        lax.broadcasted_iota(jnp.int32, (COLS, 256), 0).astype(F32) == jnp.broadcast_to(cells[1:2], (COLS, 256))
    ).astype(F32).astype(BF16)
    rows_here = (lax.broadcasted_iota(jnp.int32, (8, 256), 0) + x0).astype(F32)
    hit_x = (rows_here == jnp.broadcast_to(cells[0:1], (8, 256))).astype(F32)
    trace = jnp.concatenate([hit_x * rtrace[0, 0:1, :], hit_x * rtrace[0, 1:2, :]], axis=0)
    t_hi, t_rest = trace.astype(BF16), trace - trace.astype(BF16).astype(F32)
    t_mid, t_lo = halves(t_rest)
    surf[:, 0:16] = dot_t(hit_y, t_hi) + dot_t(hit_y, t_mid) + dot_t(hit_y, t_lo)

    z_row = lax.broadcasted_iota(jnp.int32, (COLS, DEPTH), 1)
    y_row = lax.broadcasted_iota(jnp.int32, (COLS, DEPTH), 0)
    source_cell = [jnp.broadcast_to(scell[0:1, n : n + 1], (COLS, DEPTH)) for n in range(3)]
    source_yz = (y_row == source_cell[1]) & (z_row == source_cell[2])
    source_amount = [
        jnp.where(source_yz, jnp.broadcast_to(swave[0:1, n : n + 1], (COLS, DEPTH)), 0.0) for n in range(2)
    ]
    rec_mark = z_row == ZREC
    back_w = [None] + [jnp.where(z_row[0:8] >= k, COEFFS[k], 0.0) for k in range(1, 5)]
    fore_w = [None] + [jnp.where(z_row[0:8] < DEPTH - k, COEFFS[k], 0.0) for k in range(1, 5)]

    def tall(w):
        return jnp.broadcast_to(w[0:1], (COLS, DEPTH))

    def lap_row(field, i):
        center = field[i + 4, every, :]
        out = (3.0 * COEFFS[0]) * center
        for k in range(1, 5):
            out = out + COEFFS[k] * (
                (field[i + 4 + k, every, :] + field[i + 4 - k, every, :])
                + (field[i + 4, pl.ds(PAD + k, COLS), :] + field[i + 4, pl.ds(PAD - k, COLS), :])
            )
            out = out + pltpu.roll(center, k, 1) * tall(back_w[k])
            out = out + pltpu.roll(center, DEPTH - k, 1) * tall(fore_w[k])
        return center, out

    def source(i, step):
        return jnp.where(source_cell[0] == x0 + i, source_amount[step], 0.0)

    def receivers(i, step):
        column = pltpu.roll(surf[...], (DEPTH + ZREC - step * 8 - i) % DEPTH, 1)
        return jnp.where(rec_mark, column, 0.0)

    for copy in v1:
        copy.wait_recv()
    v2 = [
        send(vg.at[:, own, :], vg.at[:, own, :], s_v2.at[k - 1], r_v2.at[k - 1], xc_peer(k)) for k in range(1, 8)
    ]

    halo_q0 = halo(q0, 2)
    halo_wait(p0, halo_p0)

    def forward_0(i, carry):
        center, lap = lap_row(p0, i)
        lap0[i] = lap
        p1[i + 4, every, :] = 2.0 * center - wb[0, i].astype(F32) + source(i, 0)
        return carry

    lax.fori_loop(0, ROWS, forward_0, 0)

    def adjoint_0(i, carry):
        center, lap = lap_row(q0, i)
        lapq[i] = lap
        q1[i + 4, every, :] = 2.0 * center - ab[0, i].astype(F32) + receivers(i, 0)
        return carry

    halo_wait(q0, halo_q0)
    lax.fori_loop(0, ROWS, adjoint_0, 0)

    for copy in v2:
        copy.wait_recv()
    for slot in range(4):
        columns = pl.ds(pl.multiple_of(lax.rem(zh + (4 - behind[slot]), 4) * 16, 16), 16)
        for i in range(ROWS):
            vfull[i, columns, :] = vg.at[slot][pl.ds(i, 16, stride=8), :]
    p1[4:12, every, :] = p1[4:12, every, :] + vfull[...] * lap0[...]
    halo_p1 = halo(p1, 4)
    q1[4:12, every, :] = q1[4:12, every, :] + vfull[...] * lapq[...]
    halo_q1 = halo(q1, 6)
    hv = around_sends(hb_vel, s_hv, r_hv)

    halo_wait(p1, halo_p1)

    def forward_1(i, carry):
        center, lap = lap_row(p1, i)
        fresh = 2.0 * center - p0[i + 4, every, :] + vfull[i] * lap + source(i, 1)
        nw[0, i] = fresh.astype(BF16)
        imgacc[i] = lap * q1[i + 4, every, :]
        return carry

    lax.fori_loop(0, ROWS, forward_1, 0)

    halo_wait(q1, halo_q1)

    def adjoint_1(i, carry):
        center, lap = lap_row(q1, i)
        fresh = 2.0 * center - q0[i + 4, every, :] + vfull[i] * lap + receivers(i, 1)
        imgacc[i] = imgacc[i] + lap0[i] * fresh
        return carry

    lax.fori_loop(0, ROWS, adjoint_1, 0)
    for z in range(4):
        for i in range(ROWS):
            imgt.at[z][pl.ds(i, 16, stride=8), :] = imgacc[i, z * 16 : (z + 1) * 16, :]

    sends_a = [
        send(
            imgt.at[:, pl.ds(pl.multiple_of(lax.rem(xc + k, 8) * 16, 16), 16), :], ra.at[k - 1],
            s_a.at[k - 1], r_a.at[k - 1], xc_peer(k),
        )
        for k in range(1, 8)
    ]
    settle(7)

    for copy in loads[9:]:
        copy.wait()
    lane = lax.broadcasted_iota(jnp.int32, (16, HID), 1)
    tile = lane >> 7
    hid_y = (tile >= 12).astype(jnp.int32) + (tile >= 24).astype(jnp.int32) + (tile >= 36).astype(jnp.int32)
    hid_x = tile - 12 * hid_y
    cell_x = hid_x + (x0 - 1)
    cell_y = hid_y + (2 * shot - 1)
    mask[...] = (
        (hid_x < 10) & (cell_x >= 0) & (cell_x < GRID_X) & (cell_y >= 0) & (cell_y < GRID_Y)
    ).astype(F32)
    gs[...] = jnp.where(lax.broadcasted_iota(jnp.int32, (TILES * 8, DEPTH), 0) % 8 == 6, 1.0, 0.0)
    rs[...] = jnp.zeros((TILES * 8, DEPTH), F32)
    ok_shot = {-1: shot > 0, 0: None, 1: shot < N_SHOT - 1}
    ok_sub = {-1: sub > 0, 0: None, 1: sub < N_SUB - 1}

    def channel(which, piece):
        for d in (-1, 0, 1):
            for e in (-1, 0, 1):
                for j in range(2):
                    block = piece(d, e, j)
                    for ok in (ok_shot[d], ok_sub[e]):
                        if ok is not None:
                            block = block * jnp.where(ok, 1.0, 0.0)
                    row = (2 + 2 * d + j) * WIDE + (0, 2, 10)[e + 1]
                    ext[row : row + block.shape[0], :] = block
        value = ext[...]
        for dz in range(3):
            gs[pl.ds(which * 3 + dz, 72, stride=8), :] = shifted(value, dz - 1)

    def velocity_piece(d, e, j):
        first = j * 8 + (6 if e == -1 else 0)
        block = hb_vel[(d + 1) * 3 + (e + 1), first : first + (8 if e == 0 else 2), :]
        return (block - CENTER_SHIFT) * CENTER_GAIN

    for copy in hv:
        copy.wait_recv()
    channel(1, velocity_piece)

    wt[...] = jnp.zeros((80, DEPTH), F32)
    kt[...] = jnp.zeros((80, DEPTH), F32)
    for n in range(9):
        for i in range(2):
            wt[n * 8 + i * 3 : n * 8 + i * 3 + 3, 0:16] = w1_own[n // 3, n % 3, :, i, :]
        kt[n * 8 : n * 8 + 3, 0:16] = k2_own[n // 3, n % 3, :, 0, :]
    wt[38:39, 0:16] = b1[...]
    w1_hi, w1_lo = halves(wt[:, 0:16])
    k2_hi, k2_lo = halves(kt[:, 0:16])
    unit = (
        lax.broadcasted_iota(jnp.int32, (16, 16), 0) == lax.broadcasted_iota(jnp.int32, (16, 16), 1)
    ).astype(F32).astype(BF16)

    def turn(x):
        return dot_t(unit, x).astype(BF16)

    w1_cat = jnp.concatenate([turn(w1_hi), turn(w1_hi), turn(w1_lo)], axis=1)
    k2_cat = jnp.concatenate([turn(k2_hi), turn(k2_hi), turn(k2_lo)], axis=1)
    k2t_cat = jnp.concatenate([k2_hi, k2_hi, k2_lo], axis=1)

    total = imgt[:, own, :]
    for k in range(1, 8):
        sends_a[k - 1].wait_recv()
        total = total + ra[k - 1]
    acca[...] = total
    for side, first in enumerate((0, 6)):
        for j in range(2):
            edge[side, :, 2 * j : 2 * j + 2, :] = total[:, 8 * j + first : 8 * j + first + 2, :]
    sends_b = []
    for n, (k, d, e) in enumerate(users):
        z = lax.rem(zh + k, 4)
        source_ref = acca.at[z] if e == 0 else edge.at[(e + 1) // 2, z]
        target_ref = whole.at[1 - d, k] if e == 0 else sides.at[(1 - e) // 2, 1 - d, k]
        sends_b.append(send(source_ref, target_ref, s_b.at[n], r_b.at[n], user(k, d, e)))
    whole[1, 0] = acca[zh]
    settle(len(users))
    for copy in sends_b:
        copy.wait_recv()
    image, image_edge = {}, {}
    for d in (-1, 0, 1):
        parts = [whole[d + 1, k] for k in range(4)]
        image[d] = ((parts[0] + parts[1]) + (parts[2] + parts[3])) * (1.0 / N_SHOT)
        for e in (-1, 1):
            parts = [sides[(e + 1) // 2, d + 1, k] for k in range(4)]
            image_edge[d, e] = ((parts[0] + parts[1]) + (parts[2] + parts[3])) * (1.0 / N_SHOT)

    def image_piece(d, e, j):
        if e == 0:
            return image[d][j * 8 : (j + 1) * 8]
        return image_edge[d, e][j * 2 : (j + 1) * 2]

    channel(0, image_piece)

    def spread(source_ref, target_ref):
        for t in range(TILES):
            target_ref[:, t * DEPTH : (t + 1) * DEPTH] = source_ref[t * 8 : (t + 1) * 8, :]

    def stacked(ref, offsets, start):
        parts = [ref[:, start + o * DEPTH : start + o * DEPTH + CHUNK] for o in offsets]
        return jnp.concatenate(parts, axis=0)

    spread(gs, g2)
    for start in range(0, HID, CHUNK):
        here = slice(start, start + CHUNK)
        f_hi, f_lo = halves(stacked(g2, OFFSETS + (0,), start))
        fhi[:, here] = f_hi
        flo[:, here] = f_lo
        pre = dot(w1_cat, jnp.concatenate([f_hi, f_lo, f_hi], axis=0))
        hidden = jnp.tanh(pre) * mask[:, here]
        hid[:, here] = hidden
        h_hi, h_lo = halves(hidden)
        smat[:, here] = dot(k2t_cat, jnp.concatenate([h_hi, h_lo, h_hi], axis=0))

    span = 20 * DEPTH
    turned = smat[0:8, 0:span]
    for n in range(1, 9):
        turned = turned + smat[n * 8 : n * 8 + 8, OFFSETS[n] * DEPTH : OFFSETS[n] * DEPTH + span]
    for t in range(20):
        tt[t * 8 : t * 8 + 8, :] = turned[:, t * DEPTH : (t + 1) * DEPTH]
    bias_sum = jnp.zeros((8, DEPTH), F32)
    for j in range(2):
        update = b2[0]
        for dz in range(3):
            update = update + shifted(tt[pl.ds(j * WIDE * 8 + dz, 8, stride=8), :], dz - 1)
        fresh = hb_vel[4, j * 8 : (j + 1) * 8, :] - update
        nv[:, j, :] = fresh
        slope = tgt[:, j, :] - fresh
        bias_sum = bias_sum + slope
        for dz in range(3):
            rs[pl.ds(((j + 2) * WIDE + 2) * 8 + dz, 8, stride=8), :] = shifted(slope, 1 - dz)

    spread(rs, r2)
    offsets_r = tuple((2 - dy) * WIDE + (2 - dx) for dx in range(3) for dy in range(3)) + (0,)
    grad_1 = jnp.zeros((32, 160), F32)
    grad_2 = jnp.zeros((32, 160), F32)
    for start in range(0, HID, CHUNK):
        here = slice(start, start + CHUNK)
        r_hi, r_lo = halves(stacked(r2, offsets_r, start))
        slope_h = dot(k2_cat, jnp.concatenate([r_hi, r_lo, r_hi], axis=0))
        hidden = hid[:, here]
        h_hi, h_lo = halves(hidden)
        grad_2 = grad_2 + dot_t(jnp.concatenate([h_hi, h_lo], axis=0), jnp.concatenate([r_hi, r_lo], axis=0))
        d_hi, d_lo = halves(slope_h * (1.0 - hidden * hidden) * mask[:, here])
        grad_1 = grad_1 + dot_t(
            jnp.concatenate([d_hi, d_lo], axis=0), jnp.concatenate([fhi[:, here], flo[:, here]], axis=0)
        )

    def joined(grad):
        value = (grad[0:16, 0:80] + grad[0:16, 80:160]) + grad[16:32, 0:80]
        return jnp.concatenate([value, jnp.zeros((16, 48), F32)], axis=1)

    gk1, gk2 = joined(grad_1), joined(grad_2)
    col = lax.broadcasted_iota(jnp.int32, (16, DEPTH), 1)
    row = lax.broadcasted_iota(jnp.int32, (16, DEPTH), 0)
    pack = jnp.where((col < 72) & ((col % 8 < 6) | (col == 38)), gk1, 0.0)
    for n in range(9):
        moved = pltpu.roll(gk2, 72 + 3 * n - 8 * n, 1)
        pack = jnp.where((col >= 72 + 3 * n) & (col < 75 + 3 * n), moved, pack)
    bias = jnp.sum(jnp.sum(bias_sum, axis=0, keepdims=True), axis=1, keepdims=True)
    pack = jnp.where((col == 99) & (row == 0), jnp.broadcast_to(bias, (16, DEPTH)), pack)

    for level, (me, peer) in enumerate(((xc, xc_peer), (zz, z_peer), (yy, y_peer))):
        re[level, me] = pack
        copies = [
            send(
                re.at[level, me], re.at[level, me], s_e.at[level * 7 + k - 1], r_e.at[level * 7 + k - 1], peer(k)
            )
            for k in range(1, 8)
        ]
        settle(7)
        for copy in copies:
            copy.wait_recv()
        pack = re[level, 0]
        for n in range(1, 8):
            pack = pack + re[level, n]

    squares = jnp.sum(jnp.sum(pack * pack, axis=0, keepdims=True), axis=1, keepdims=True)
    factor = 1.0 / jnp.sqrt(squares * (1.0 / ENTRIES) + 1e-06)
    moves[...] = pack * factor

    settle()


def writer(nw, nv, moves, nw_out, nv_out, w1_out, b1_out, k2_out, b2_out, nw_own, nv_own, pack, w1_own, k2_own, sem):
    def copy(source, target, n):
        move = pltpu.make_async_copy(source, target, sem.at[n])
        move.start()
        return move

    loads = [copy(moves, pack, 0), copy(nw, nw_own, 1), copy(nv, nv_own, 2)]
    loads[0].wait()
    turned = jnp.transpose(pack[...])
    for n in range(9):
        for i in range(2):
            w1_own[n // 3, n % 3, :, i, :] = turned[n * 8 + i * 3 : n * 8 + i * 3 + 3]
        k2_own[n // 3, n % 3, :, 0, :] = turned[72 + 3 * n : 75 + 3 * n]
    b1_out[...] = turned[38:39]
    b2_out[...] = pack[0:1, 99:100]
    stores = [copy(w1_own, w1_out, 3), copy(k2_own, k2_out, 4)]
    loads[1].wait()
    stores.append(copy(nw_own, nw_out, 5))
    loads[2].wait()
    stores.append(copy(nv_own, nv_out, 6))
    for move in stores:
        move.wait()


def shards(
    wave_before, wave_now, adjoint_before, adjoint_now, velocity, target_model, source_cell, source_wave,
    receiver_cell, receiver_trace, first_kernel, first_bias, second_kernel, second_bias,
):
    operands = (
        wave_before, wave_now, adjoint_before, adjoint_now, velocity, target_model, source_cell, source_wave,
        receiver_cell.transpose(0, 2, 1), receiver_trace, first_kernel.transpose(2, 3, 4, 1, 0),
        first_bias.reshape(1, 16), second_kernel.transpose(2, 3, 4, 0, 1), second_bias,
    )
    vmem = pl.BlockSpec(memory_space=pltpu.VMEM)
    hbm = pl.BlockSpec(memory_space=pltpu.HBM)
    dma = pltpu.SemaphoreType.DMA
    field = pltpu.VMEM((16, COLS + 2 * PAD, DEPTH), F32)
    block = pltpu.VMEM((ROWS, COLS, DEPTH), F32)
    scratch = [pltpu.VMEM(x.shape, x.dtype) for x in operands[:-1]] + [pltpu.SMEM((1,), F32)] + [
        field, field, field, field, block, block, block, block,
        pltpu.VMEM((4, DEPTH, DEPTH), F32),
        pltpu.VMEM((COLS, DEPTH), F32),
        pltpu.VMEM((4, DEPTH, DEPTH), F32),
        pltpu.VMEM((7, 4, 16, DEPTH), F32),
        pltpu.VMEM((4, 16, DEPTH), F32),
        pltpu.VMEM((2, 4, 4, DEPTH), F32),
        pltpu.VMEM((3, 4, 16, DEPTH), F32),
        pltpu.VMEM((2, 3, 4, 4, DEPTH), F32),
        pltpu.VMEM((9, 16, DEPTH), F32),
        pltpu.VMEM((72, DEPTH), F32),
        pltpu.VMEM((TILES * 8, DEPTH), F32),
        pltpu.VMEM((8, TILES * DEPTH), F32),
        pltpu.VMEM((TILES * 8, DEPTH), F32),
        pltpu.VMEM((8, TILES * DEPTH), F32),
        pltpu.VMEM((80, HID), BF16),
        pltpu.VMEM((80, HID), BF16),
        pltpu.VMEM((16, HID), F32),
        pltpu.VMEM((80, HID), F32),
        pltpu.VMEM((160, DEPTH), F32),
        pltpu.VMEM((16, HID), F32),
        pltpu.VMEM((3, 8, 16, DEPTH), F32),
        pltpu.VMEM((80, DEPTH), F32),
        pltpu.VMEM((80, DEPTH), F32),
        dma((len(operands),)),
    ]
    for count in (8, 3, 7, 8, 7, 35, 21):
        scratch += [dma((count,)), dma((count,))]
    next_wave, new_velocity, moves = pl.pallas_call(
        kernel,
        out_shape=(
            jax.ShapeDtypeStruct(wave_now.shape, BF16),
            jax.ShapeDtypeStruct(velocity.shape, F32),
            jax.ShapeDtypeStruct((16, DEPTH), F32),
        ),
        in_specs=[hbm] * len(operands),
        out_specs=(vmem, vmem, vmem),
        scratch_shapes=scratch,
        compiler_params=pltpu.CompilerParams(
            collective_id=0, has_side_effects=True, vmem_limit_bytes=60 * 1024 * 1024
        ),
    )(*operands)
    outs = (
        jax.ShapeDtypeStruct(wave_now.shape, BF16),
        jax.ShapeDtypeStruct(velocity.shape, F32),
        jax.ShapeDtypeStruct((3, 3, 3, 2, 16), F32),
        jax.ShapeDtypeStruct((1, 16), F32),
        jax.ShapeDtypeStruct((3, 3, 3, 1, 16), F32),
        jax.ShapeDtypeStruct((1, 1), F32),
    )
    next_wave, new_velocity, w1, b1, k2, b2 = pl.pallas_call(
        writer,
        out_shape=outs,
        in_specs=[hbm, hbm, hbm],
        out_specs=(hbm, hbm, hbm, vmem, hbm, vmem),
        scratch_shapes=[
            pltpu.VMEM(outs[0].shape, BF16), pltpu.VMEM(outs[1].shape, F32), pltpu.VMEM((16, DEPTH), F32),
            pltpu.VMEM(outs[2].shape, F32), pltpu.VMEM(outs[4].shape, F32), dma((7,)),
        ],
    )(next_wave, new_velocity, moves)
    return (
        next_wave,
        new_velocity,
        w1.transpose(4, 3, 0, 1, 2),
        b1.reshape(16),
        k2.transpose(3, 4, 0, 1, 2),
        b2.reshape(1),
    )


def solution(mesh):
    return jax.shard_map(
        shards,
        mesh=mesh,
        in_specs=(
            P("shot", "sub", None, None),
            P("shot", "sub", None, None),
            P("shot", "sub", None, None),
            P("shot", "sub", None, None),
            P("sub", "shot", None),
            P("sub", "shot", None),
            P("shot", None),
            P("shot", None),
            P("shot", None, None),
            P("shot", None, None),
            P(),
            P(),
            P(),
            P(),
        ),
        out_specs=(P("shot", "sub", None, None), P("sub", "shot", None), P(), P(), P(), P()),
        check_vma=False,
    )
```

```python
import functools

import jax
import jax.numpy as jnp
from jax import lax
from jax.experimental import pallas as pl
from jax.experimental.pallas import tpu as pltpu
from jax.sharding import PartitionSpec as P

F32 = jnp.float32
BF16 = jnp.bfloat16
MESH = pl.DeviceIdType.MESH

ZREC = 2
COEFFS = (-205.0 / 72.0, 8.0 / 5.0, -1.0 / 5.0, 8.0 / 315.0, -1.0 / 560.0)
CENTER_SHIFT = 0.125
CENTER_GAIN = 16.0
ENTRIES = 1313

ROWS = 8
COLS = 64
DEPTH = 128
PAD = 8
N_SHOT, N_SUB = 32, 16
GRID_X, GRID_Y = 128, 64

TILES = 80
WIDE = 12
HID = 48 * DEPTH
CHUNK = 8 * DEPTH
FAR_FIRST = (4, 3, 5, 2, 6, 1, 7)
OFFSETS = tuple(dy * WIDE + dx for dx in range(3) for dy in range(3))
BLOCKS = 10


def dot(a, b):
    return jnp.dot(a, b, preferred_element_type=F32)


def dot_t(a, b):
    return lax.dot_general(a, b, (((1,), (1,)), ((), ())), preferred_element_type=F32)


def halves(x):
    high = x.astype(BF16)
    return high, (x - high.astype(F32)).astype(BF16)


def shifted(x, dz):
    if dz == 0:
        return x
    z = lax.broadcasted_iota(jnp.int32, x.shape, 1)
    if dz > 0:
        return jnp.where(z < DEPTH - dz, pltpu.roll(x, DEPTH - dz, 1), 0.0)
    return jnp.where(z >= -dz, pltpu.roll(x, -dz, 1), 0.0)


def kernel(
    wb_in, wn_in, ab_in, an_in, vel_in, tgt_in, scell_in, swave_in, rcell_in, rtrace_in, w1_in, b1_in, k2_in, b2_in,
    nw, nv, moves,
    wb, wn, ab, an, vel, tgt, scell, swave, rcell, rtrace, w1_own, b1, k2_own, b2,
    p0, q0, p1, q1, lap0, lapq, imgacc, vfull, vg, surf, imgt, ra, acca, edge, whole, sides, hb_vel,
    ext, gs, g2, rs, r2, fhi, flo, hid, smat, tt, mask, re, wt, kt,
    s_in, s_hal, r_hal, s_v1, r_v1, s_v2, r_v2, s_hv, r_hv, s_a, r_a, s_b, r_b, s_e, r_e,
):
    shot = lax.axis_index("shot")
    sub = lax.axis_index("sub")
    zh, xc = lax.div(shot, 8), lax.rem(shot, 8)
    zlo, yy = lax.div(sub, 8), lax.rem(sub, 8)
    zz = zh * 2 + zlo
    x0 = sub * ROWS
    up, down = lax.rem(sub + 1, N_SUB), lax.rem(sub + (N_SUB - 1), N_SUB)

    def xc_peer(k):
        return (zh * 8 + lax.rem(xc + k, 8), sub)

    def zh_peer(k):
        return (lax.rem(zh + k, 4) * 8 + xc, sub)

    def z_peer(k):
        z = lax.rem(zz + k, 8)
        return (lax.div(z, 2) * 8 + xc, lax.rem(z, 2) * 8 + yy)

    def y_peer(k):
        return (shot, zlo * 8 + lax.rem(yy + k, 8))

    def near(d, e):
        return (lax.rem(shot + (d + N_SHOT), N_SHOT), lax.rem(sub + (e + N_SUB), N_SUB))

    around = [(d, e) for d in (-1, 0, 1) for e in (-1, 0, 1) if (d, e) != (0, 0)]
    def user(k, d, e):
        owner = lax.rem(zh + k, 4) * 8 + xc
        return (lax.rem(owner + (d + N_SHOT), N_SHOT), lax.rem(sub + (e + N_SUB), N_SUB))

    users = [(k, d, e) for k in (2, 1, 3, 0) for d in (1, -1, 0) for e in (1, -1, 0) if (k, d, e) != (0, 0, 0)]
    twin = (shot, lax.rem(sub + 8, N_SUB))
    greeted = [xc_peer(k) for k in range(1, 8)] + [zh_peer(k) for k in range(1, 4)] + [twin]
    greeted += [near(d, e) for d, e in around]
    loads = [
        pltpu.make_async_copy(outer, inner, s_in.at[n])
        for n, (outer, inner) in enumerate((
            (vel_in, vel), (wn_in, wn), (an_in, an), (wb_in, wb), (ab_in, ab), (rcell_in, rcell),
            (rtrace_in, rtrace), (scell_in, scell), (swave_in, swave), (tgt_in, tgt), (w1_in, w1_own),
            (b1_in, b1), (k2_in, k2_own), (b2_in, b2),
        ))
    ]
    loads[0].start()
    barrier = pltpu.get_barrier_semaphore()
    for device in greeted:
        pl.semaphore_signal(barrier, inc=1, device_id=device, device_id_type=MESH)
    for copy in loads[1:]:
        copy.start()

    pending = []

    def settle(keep=0):
        for copy in pending[: len(pending) - keep]:
            copy.wait_send()
        del pending[: len(pending) - keep]

    def send(src, dst, ssem, rsem, device):
        copy = pltpu.make_async_remote_copy(
            src_ref=src, dst_ref=dst, send_sem=ssem, recv_sem=rsem, device_id=device, device_id_type=MESH
        )
        copy.start()
        pending.append(copy)
        return copy

    loads[0].wait()
    for j in range(2):
        hb_vel[4, j * 8 : (j + 1) * 8, :] = vel[:, j, :]
    own = pl.ds(pl.multiple_of(xc * 16, 16), 16)

    pl.semaphore_wait(barrier, len(greeted))

    every = pl.ds(PAD, COLS)

    def halo(field, index, columns=every):
        return [
            send(
                field.at[pl.ds(8, 4), columns, :], field.at[pl.ds(0, 4), columns, :],
                s_hal.at[index], r_hal.at[index], (shot, up),
            ),
            send(
                field.at[pl.ds(4, 4), columns, :], field.at[pl.ds(12, 4), columns, :],
                s_hal.at[index + 1], r_hal.at[index + 1], (shot, down),
            ),
        ]

    def halo_wait(field, copies):
        for copy in copies:
            copy.wait_recv()

        @pl.when(sub == 0)
        def _():
            field[0:4, PAD : PAD + COLS, :] = jnp.zeros((4, COLS, DEPTH), F32)

        @pl.when(sub == N_SUB - 1)
        def _():
            field[12:16, PAD : PAD + COLS, :] = jnp.zeros((4, COLS, DEPTH), F32)

    behind = (0, 1, 3, 2)
    v1 = [
        send(hb_vel.at[4], vg.at[slot, own, :], s_v1.at[slot - 1], r_v1.at[slot - 1], zh_peer(behind[slot]))
        for slot in (3, 1, 2)
    ]

    vg[0, own, :] = hb_vel[4]

    loads[1].wait()
    p0[4:12, every, :] = wn[0].astype(F32)
    halo_p0 = halo(p0, 0)
    loads[2].wait()
    q0[4:12, every, :] = an[0].astype(F32)
    zeros_pad = jnp.zeros((16, PAD, DEPTH), F32)
    for field in (p0, q0, p1, q1):
        field[:, 0:PAD, :] = zeros_pad
        field[:, PAD + COLS :, :] = zeros_pad

    def around_sends(buffer, ssem, rsem):
        return [
            send(
                buffer.at[4], buffer.at[(1 - d) * 3 + (1 - e)], ssem.at[n], rsem.at[n], near(d, e)
            )
            for n, (d, e) in enumerate(around)
        ]

    for copy in loads[3:9]:
        copy.wait()
    cells = rcell[0].astype(F32)
    hit_y = (
        lax.broadcasted_iota(jnp.int32, (COLS, 256), 0).astype(F32) == jnp.broadcast_to(cells[1:2], (COLS, 256))
    ).astype(F32).astype(BF16)
    rows_here = (lax.broadcasted_iota(jnp.int32, (8, 256), 0) + x0).astype(F32)
    hit_x = (rows_here == jnp.broadcast_to(cells[0:1], (8, 256))).astype(F32)
    trace = jnp.concatenate([hit_x * rtrace[0, 0:1, :], hit_x * rtrace[0, 1:2, :]], axis=0)
    t_hi, t_rest = trace.astype(BF16), trace - trace.astype(BF16).astype(F32)
    t_mid, t_lo = halves(t_rest)
    surf[:, 0:16] = dot_t(hit_y, t_hi) + dot_t(hit_y, t_mid) + dot_t(hit_y, t_lo)

    z_row = lax.broadcasted_iota(jnp.int32, (COLS, DEPTH), 1)
    y_row = lax.broadcasted_iota(jnp.int32, (COLS, DEPTH), 0)
    source_cell = [jnp.broadcast_to(scell[0:1, n : n + 1], (COLS, DEPTH)) for n in range(3)]
    source_yz = (y_row == source_cell[1]) & (z_row == source_cell[2])
    source_amount = [
        jnp.where(source_yz, jnp.broadcast_to(swave[0:1, n : n + 1], (COLS, DEPTH)), 0.0) for n in range(2)
    ]
    rec_mark = z_row == ZREC
    back_w = [None] + [jnp.where(z_row[0:8] >= k, COEFFS[k], 0.0) for k in range(1, 5)]
    fore_w = [None] + [jnp.where(z_row[0:8] < DEPTH - k, COEFFS[k], 0.0) for k in range(1, 5)]

    def tall(w):
        return jnp.broadcast_to(w[0:1], (COLS, DEPTH))

    def lap_row(field, i):
        center = field[i + 4, every, :]
        out = (3.0 * COEFFS[0]) * center
        for k in range(1, 5):
            out = out + COEFFS[k] * (
                (field[i + 4 + k, every, :] + field[i + 4 - k, every, :])
                + (field[i + 4, pl.ds(PAD + k, COLS), :] + field[i + 4, pl.ds(PAD - k, COLS), :])
            )
            out = out + pltpu.roll(center, k, 1) * tall(back_w[k])
            out = out + pltpu.roll(center, DEPTH - k, 1) * tall(fore_w[k])
        return center, out

    def source(i, step):
        return jnp.where(source_cell[0] == x0 + i, source_amount[step], 0.0)

    def receivers(i, step):
        column = pltpu.roll(surf[...], (DEPTH + ZREC - step * 8 - i) % DEPTH, 1)
        return jnp.where(rec_mark, column, 0.0)

    for copy in v1:
        copy.wait_recv()
    v2 = [
        send(vg.at[:, own, :], vg.at[:, own, :], s_v2.at[k - 1], r_v2.at[k - 1], xc_peer(k)) for k in FAR_FIRST
    ]

    halo_q0 = halo(q0, 2)
    halo_wait(p0, halo_p0)

    def forward_0(i, carry):
        center, lap = lap_row(p0, i)
        lap0[i] = lap
        p1[i + 4, every, :] = 2.0 * center - wb[0, i].astype(F32) + source(i, 0)
        return carry

    lax.fori_loop(0, ROWS, forward_0, 0)

    def adjoint_0(i, carry):
        center, lap = lap_row(q0, i)
        lapq[i] = lap
        q1[i + 4, every, :] = 2.0 * center - ab[0, i].astype(F32) + receivers(i, 0)
        return carry

    halo_wait(q0, halo_q0)
    lax.fori_loop(0, ROWS, adjoint_0, 0)

    for copy in v2:
        copy.wait_recv()
    for slot in range(4):
        columns = pl.ds(pl.multiple_of(lax.rem(zh + (4 - behind[slot]), 4) * 16, 16), 16)
        for i in range(ROWS):
            vfull[i, columns, :] = vg.at[slot][pl.ds(i, 16, stride=8), :]
    p1[4:12, every, :] = p1[4:12, every, :] + vfull[...] * lap0[...]
    halo_p1 = halo(p1, 4)
    q1[4:12, every, :] = q1[4:12, every, :] + vfull[...] * lapq[...]
    halo_q1 = halo(q1, 6)

    halo_wait(p1, halo_p1)
    hv = around_sends(hb_vel, s_hv, r_hv)

    def forward_1(i, carry):
        center, lap = lap_row(p1, i)
        fresh = 2.0 * center - p0[i + 4, every, :] + vfull[i] * lap + source(i, 1)
        nw[0, i] = fresh.astype(BF16)
        imgacc[i] = lap * q1[i + 4, every, :]
        return carry

    lax.fori_loop(0, ROWS, forward_1, 0)

    halo_wait(q1, halo_q1)

    def adjoint_1(i, carry):
        center, lap = lap_row(q1, i)
        fresh = 2.0 * center - q0[i + 4, every, :] + vfull[i] * lap + receivers(i, 1)
        imgacc[i] = imgacc[i] + lap0[i] * fresh
        return carry

    lax.fori_loop(0, ROWS, adjoint_1, 0)
    for z in range(4):
        for i in range(ROWS):
            imgt.at[z][pl.ds(i, 16, stride=8), :] = imgacc[i, z * 16 : (z + 1) * 16, :]

    sends_a = {
        k: send(
            imgt.at[:, pl.ds(pl.multiple_of(lax.rem(xc + k, 8) * 16, 16), 16), :], ra.at[k - 1],
            s_a.at[k - 1], r_a.at[k - 1], xc_peer(k),
        )
        for k in FAR_FIRST
    }
    settle(7)

    for copy in loads[9:]:
        copy.wait()
    lane = lax.broadcasted_iota(jnp.int32, (16, HID), 1)
    tile = lane >> 7
    hid_y = (tile >= 12).astype(jnp.int32) + (tile >= 24).astype(jnp.int32) + (tile >= 36).astype(jnp.int32)
    hid_x = tile - 12 * hid_y
    cell_x = hid_x + (x0 - 1)
    cell_y = hid_y + (2 * shot - 1)
    mask[...] = (
        (hid_x < 10) & (cell_x >= 0) & (cell_x < GRID_X) & (cell_y >= 0) & (cell_y < GRID_Y)
    ).astype(F32)
    gs[...] = jnp.where(lax.broadcasted_iota(jnp.int32, (TILES * 8, DEPTH), 0) % 8 == 6, 1.0, 0.0)
    rs[...] = jnp.zeros((TILES * 8, DEPTH), F32)
    ok_shot = {-1: shot > 0, 0: None, 1: shot < N_SHOT - 1}
    ok_sub = {-1: sub > 0, 0: None, 1: sub < N_SUB - 1}

    def channel(which, piece):
        for d in (-1, 0, 1):
            for e in (-1, 0, 1):
                for j in range(2):
                    block = piece(d, e, j)
                    for ok in (ok_shot[d], ok_sub[e]):
                        if ok is not None:
                            block = block * jnp.where(ok, 1.0, 0.0)
                    row = (2 + 2 * d + j) * WIDE + (0, 2, 10)[e + 1]
                    ext[row : row + block.shape[0], :] = block
        value = ext[...]
        for dz in range(3):
            gs[pl.ds(which * 3 + dz, 72, stride=8), :] = shifted(value, dz - 1)

    def velocity_piece(d, e, j):
        first = j * 8 + (6 if e == -1 else 0)
        block = hb_vel[(d + 1) * 3 + (e + 1), first : first + (8 if e == 0 else 2), :]
        return (block - CENTER_SHIFT) * CENTER_GAIN

    for copy in hv:
        copy.wait_recv()
    channel(1, velocity_piece)

    wt[...] = jnp.zeros((80, DEPTH), F32)
    kt[...] = jnp.zeros((80, DEPTH), F32)
    for n in range(9):
        for i in range(2):
            wt[n * 8 + i * 3 : n * 8 + i * 3 + 3, 0:16] = w1_own[n // 3, n % 3, :, i, :]
        kt[n * 8 : n * 8 + 3, 0:16] = k2_own[n // 3, n % 3, :, 0, :]
    wt[38:39, 0:16] = b1[...]
    w1_hi, w1_lo = halves(wt[:, 0:16])
    k2_hi, k2_lo = halves(kt[:, 0:16])
    unit = (
        lax.broadcasted_iota(jnp.int32, (16, 16), 0) == lax.broadcasted_iota(jnp.int32, (16, 16), 1)
    ).astype(F32).astype(BF16)

    def turn(x):
        return dot_t(unit, x).astype(BF16)

    w1_cat = jnp.concatenate([turn(w1_hi), turn(w1_hi), turn(w1_lo)], axis=1)
    k2_cat = jnp.concatenate([turn(k2_hi), turn(k2_hi), turn(k2_lo)], axis=1)
    k2t_cat = jnp.concatenate([k2_hi, k2_hi, k2_lo], axis=1)

    total = imgt[:, own, :]
    for k in range(1, 8):
        sends_a[k].wait_recv()
        total = total + ra[k - 1]
    acca[...] = total
    for side, first in enumerate((0, 6)):
        for j in range(2):
            edge[side, :, 2 * j : 2 * j + 2, :] = total[:, 8 * j + first : 8 * j + first + 2, :]
    sends_b = []
    for n, (k, d, e) in enumerate(users):
        z = lax.rem(zh + k, 4)
        source_ref = acca.at[z] if e == 0 else edge.at[(e + 1) // 2, z]
        target_ref = whole.at[1 - d, k] if e == 0 else sides.at[(1 - e) // 2, 1 - d, k]
        sends_b.append(send(source_ref, target_ref, s_b.at[n], r_b.at[n], user(k, d, e)))
    whole[1, 0] = acca[zh]
    settle(len(users))
    for copy in sends_b:
        copy.wait_recv()
    image, image_edge = {}, {}
    for d in (-1, 0, 1):
        parts = [whole[d + 1, k] for k in range(4)]
        image[d] = ((parts[0] + parts[1]) + (parts[2] + parts[3])) * (1.0 / N_SHOT)
        for e in (-1, 1):
            parts = [sides[(e + 1) // 2, d + 1, k] for k in range(4)]
            image_edge[d, e] = ((parts[0] + parts[1]) + (parts[2] + parts[3])) * (1.0 / N_SHOT)

    def image_piece(d, e, j):
        if e == 0:
            return image[d][j * 8 : (j + 1) * 8]
        return image_edge[d, e][j * 2 : (j + 1) * 2]

    channel(0, image_piece)

    def spread(source_ref, target_ref):
        for t in range(TILES):
            target_ref[:, t * DEPTH : (t + 1) * DEPTH] = source_ref[t * 8 : (t + 1) * 8, :]

    def stacked(ref, offsets, start):
        parts = [ref[:, start + o * DEPTH : start + o * DEPTH + CHUNK] for o in offsets]
        return jnp.concatenate(parts, axis=0)

    spread(gs, g2)
    for start in range(0, HID, CHUNK):
        here = slice(start, start + CHUNK)
        f_hi, f_lo = halves(stacked(g2, OFFSETS + (0,), start))
        fhi[:, here] = f_hi
        flo[:, here] = f_lo
        pre = dot(w1_cat, jnp.concatenate([f_hi, f_lo, f_hi], axis=0))
        hidden = jnp.tanh(pre) * mask[:, here]
        hid[:, here] = hidden
        h_hi, h_lo = halves(hidden)
        smat[:, here] = dot(k2t_cat, jnp.concatenate([h_hi, h_lo, h_hi], axis=0))

    span = 20 * DEPTH
    turned = smat[0:8, 0:span]
    for n in range(1, 9):
        turned = turned + smat[n * 8 : n * 8 + 8, OFFSETS[n] * DEPTH : OFFSETS[n] * DEPTH + span]
    for t in range(20):
        tt[t * 8 : t * 8 + 8, :] = turned[:, t * DEPTH : (t + 1) * DEPTH]
    bias_sum = jnp.zeros((8, DEPTH), F32)
    for j in range(2):
        update = b2[0]
        for dz in range(3):
            update = update + shifted(tt[pl.ds(j * WIDE * 8 + dz, 8, stride=8), :], dz - 1)
        fresh = hb_vel[4, j * 8 : (j + 1) * 8, :] - update
        nv[:, j, :] = fresh
        slope = tgt[:, j, :] - fresh
        bias_sum = bias_sum + slope
        for dz in range(3):
            rs[pl.ds(((j + 2) * WIDE + 2) * 8 + dz, 8, stride=8), :] = shifted(slope, 1 - dz)

    spread(rs, r2)
    offsets_r = tuple((2 - dy) * WIDE + (2 - dx) for dx in range(3) for dy in range(3)) + (0,)
    grad_1 = jnp.zeros((32, 160), F32)
    grad_2 = jnp.zeros((32, 160), F32)
    for start in range(0, HID, CHUNK):
        here = slice(start, start + CHUNK)
        r_hi, r_lo = halves(stacked(r2, offsets_r, start))
        slope_h = dot(k2_cat, jnp.concatenate([r_hi, r_lo, r_hi], axis=0))
        hidden = hid[:, here]
        h_hi, h_lo = halves(hidden)
        grad_2 = grad_2 + dot_t(jnp.concatenate([h_hi, h_lo], axis=0), jnp.concatenate([r_hi, r_lo], axis=0))
        d_hi, d_lo = halves(slope_h * (1.0 - hidden * hidden) * mask[:, here])
        grad_1 = grad_1 + dot_t(
            jnp.concatenate([d_hi, d_lo], axis=0), jnp.concatenate([fhi[:, here], flo[:, here]], axis=0)
        )

    def joined(grad):
        value = (grad[0:16, 0:80] + grad[0:16, 80:160]) + grad[16:32, 0:80]
        return jnp.concatenate([value, jnp.zeros((16, 48), F32)], axis=1)

    gk1, gk2 = joined(grad_1), joined(grad_2)
    col = lax.broadcasted_iota(jnp.int32, (16, DEPTH), 1)
    row = lax.broadcasted_iota(jnp.int32, (16, DEPTH), 0)
    pack = jnp.where((col < 72) & ((col % 8 < 6) | (col == 38)), gk1, 0.0)
    for n in range(9):
        moved = pltpu.roll(gk2, 72 + 3 * n - 8 * n, 1)
        pack = jnp.where((col >= 72 + 3 * n) & (col < 75 + 3 * n), moved, pack)
    bias = jnp.sum(jnp.sum(bias_sum, axis=0, keepdims=True), axis=1, keepdims=True)
    pack = jnp.where((col == 99) & (row == 0), jnp.broadcast_to(bias, (16, DEPTH)), pack)

    for level, (me, peer) in enumerate(((xc, xc_peer), (zz, z_peer), (yy, y_peer))):
        re[level, me] = pack
        copies = [
            send(
                re.at[level, me], re.at[level, me], s_e.at[level * 7 + k - 1], r_e.at[level * 7 + k - 1], peer(k)
            )
            for k in FAR_FIRST
        ]
        settle(7)
        for copy in copies:
            copy.wait_recv()
        pack = re[level, 0]
        for n in range(1, 8):
            pack = pack + re[level, n]

    squares = jnp.sum(jnp.sum(pack * pack, axis=0, keepdims=True), axis=1, keepdims=True)
    factor = 1.0 / jnp.sqrt(squares * (1.0 / ENTRIES) + 1e-06)
    moves[...] = pack * factor

    settle()


def writer(nw, nv, moves, nw_out, nv_out, w1_out, b1_out, k2_out, b2_out, nw_own, nv_own, pack, w1_own, k2_own, sem):
    def copy(source, target, n):
        move = pltpu.make_async_copy(source, target, sem.at[n])
        move.start()
        return move

    loads = [copy(moves, pack, 0), copy(nw, nw_own, 1), copy(nv, nv_own, 2)]
    loads[0].wait()
    turned = jnp.transpose(pack[...])
    for n in range(9):
        for i in range(2):
            w1_own[n // 3, n % 3, :, i, :] = turned[n * 8 + i * 3 : n * 8 + i * 3 + 3]
        k2_own[n // 3, n % 3, :, 0, :] = turned[72 + 3 * n : 75 + 3 * n]
    b1_out[...] = turned[38:39]
    b2_out[...] = pack[0:1, 99:100]
    stores = [copy(w1_own, w1_out, 3), copy(k2_own, k2_out, 4)]
    loads[1].wait()
    stores.append(copy(nw_own, nw_out, 5))
    loads[2].wait()
    stores.append(copy(nv_own, nv_out, 6))
    for move in stores:
        move.wait()


def shards(
    wave_before, wave_now, adjoint_before, adjoint_now, velocity, target_model, source_cell, source_wave,
    receiver_cell, receiver_trace, first_kernel, first_bias, second_kernel, second_bias,
):
    operands = (
        wave_before, wave_now, adjoint_before, adjoint_now, velocity, target_model, source_cell, source_wave,
        receiver_cell.transpose(0, 2, 1), receiver_trace, first_kernel.transpose(2, 3, 4, 1, 0),
        first_bias.reshape(1, 16), second_kernel.transpose(2, 3, 4, 0, 1), second_bias,
    )
    vmem = pl.BlockSpec(memory_space=pltpu.VMEM)
    hbm = pl.BlockSpec(memory_space=pltpu.HBM)
    dma = pltpu.SemaphoreType.DMA
    field = pltpu.VMEM((16, COLS + 2 * PAD, DEPTH), F32)
    block = pltpu.VMEM((ROWS, COLS, DEPTH), F32)
    scratch = [pltpu.VMEM(x.shape, x.dtype) for x in operands[:-1]] + [pltpu.SMEM((1,), F32)] + [
        field, field, field, field, block, block, block, block,
        pltpu.VMEM((4, DEPTH, DEPTH), F32),
        pltpu.VMEM((COLS, DEPTH), F32),
        pltpu.VMEM((4, DEPTH, DEPTH), F32),
        pltpu.VMEM((7, 4, 16, DEPTH), F32),
        pltpu.VMEM((4, 16, DEPTH), F32),
        pltpu.VMEM((2, 4, 4, DEPTH), F32),
        pltpu.VMEM((3, 4, 16, DEPTH), F32),
        pltpu.VMEM((2, 3, 4, 4, DEPTH), F32),
        pltpu.VMEM((9, 16, DEPTH), F32),
        pltpu.VMEM((72, DEPTH), F32),
        pltpu.VMEM((TILES * 8, DEPTH), F32),
        pltpu.VMEM((8, TILES * DEPTH), F32),
        pltpu.VMEM((TILES * 8, DEPTH), F32),
        pltpu.VMEM((8, TILES * DEPTH), F32),
        pltpu.VMEM((80, HID), BF16),
        pltpu.VMEM((80, HID), BF16),
        pltpu.VMEM((16, HID), F32),
        pltpu.VMEM((80, HID), F32),
        pltpu.VMEM((160, DEPTH), F32),
        pltpu.VMEM((16, HID), F32),
        pltpu.VMEM((3, 8, 16, DEPTH), F32),
        pltpu.VMEM((80, DEPTH), F32),
        pltpu.VMEM((80, DEPTH), F32),
        dma((len(operands),)),
    ]
    for count in (8, 3, 7, 8, 7, 35, 21):
        scratch += [dma((count,)), dma((count,))]
    next_wave, new_velocity, moves = pl.pallas_call(
        kernel,
        out_shape=(
            jax.ShapeDtypeStruct(wave_now.shape, BF16),
            jax.ShapeDtypeStruct(velocity.shape, F32),
            jax.ShapeDtypeStruct((16, DEPTH), F32),
        ),
        in_specs=[hbm] * len(operands),
        out_specs=(vmem, vmem, vmem),
        scratch_shapes=scratch,
        compiler_params=pltpu.CompilerParams(
            collective_id=0, has_side_effects=True, vmem_limit_bytes=60 * 1024 * 1024
        ),
    )(*operands)
    outs = (
        jax.ShapeDtypeStruct(wave_now.shape, BF16),
        jax.ShapeDtypeStruct(velocity.shape, F32),
        jax.ShapeDtypeStruct((3, 3, 3, 2, 16), F32),
        jax.ShapeDtypeStruct((1, 16), F32),
        jax.ShapeDtypeStruct((3, 3, 3, 1, 16), F32),
        jax.ShapeDtypeStruct((1, 1), F32),
    )
    next_wave, new_velocity, w1, b1, k2, b2 = pl.pallas_call(
        writer,
        out_shape=outs,
        in_specs=[hbm, hbm, hbm],
        out_specs=(hbm, hbm, hbm, vmem, hbm, vmem),
        scratch_shapes=[
            pltpu.VMEM(outs[0].shape, BF16), pltpu.VMEM(outs[1].shape, F32), pltpu.VMEM((16, DEPTH), F32),
            pltpu.VMEM(outs[2].shape, F32), pltpu.VMEM(outs[4].shape, F32), dma((7,)),
        ],
    )(next_wave, new_velocity, moves)
    return (
        next_wave,
        new_velocity,
        w1.transpose(4, 3, 0, 1, 2),
        b1.reshape(16),
        k2.transpose(3, 4, 0, 1, 2),
        b2.reshape(1),
    )


def solution(mesh):
    return jax.shard_map(
        shards,
        mesh=mesh,
        in_specs=(
            P("shot", "sub", None, None),
            P("shot", "sub", None, None),
            P("shot", "sub", None, None),
            P("shot", "sub", None, None),
            P("sub", "shot", None),
            P("sub", "shot", None),
            P("shot", None),
            P("shot", None),
            P("shot", None, None),
            P("shot", None, None),
            P(),
            P(),
            P(),
            P(),
        ),
        out_specs=(P("shot", "sub", None, None), P("sub", "shot", None), P(), P(), P(), P()),
        check_vma=False,
    )
```

```python
import functools

import jax
import jax.numpy as jnp
from jax import lax
from jax.experimental import pallas as pl
from jax.experimental.pallas import tpu as pltpu
from jax.sharding import PartitionSpec as P

F32 = jnp.float32
BF16 = jnp.bfloat16
MESH = pl.DeviceIdType.MESH

ZREC = 2
COEFFS = (-205.0 / 72.0, 8.0 / 5.0, -1.0 / 5.0, 8.0 / 315.0, -1.0 / 560.0)
CENTER_SHIFT = 0.125
CENTER_GAIN = 16.0
ENTRIES = 1313

ROWS = 8
COLS = 64
DEPTH = 128
PAD = 8
N_SHOT, N_SUB = 32, 16
GRID_X, GRID_Y = 128, 64

TILES = 80
WIDE = 12
HID = 48 * DEPTH
CHUNK = 8 * DEPTH
FAR_FIRST = (4, 3, 5, 2, 6, 1, 7)
OFFSETS = tuple(dy * WIDE + dx for dx in range(3) for dy in range(3))
BLOCKS = 10


def dot(a, b):
    return jnp.dot(a, b, preferred_element_type=F32)


def dot_t(a, b):
    return lax.dot_general(a, b, (((1,), (1,)), ((), ())), preferred_element_type=F32)


def halves(x):
    high = x.astype(BF16)
    return high, (x - high.astype(F32)).astype(BF16)


def shifted(x, dz):
    if dz == 0:
        return x
    z = lax.broadcasted_iota(jnp.int32, x.shape, 1)
    if dz > 0:
        return jnp.where(z < DEPTH - dz, pltpu.roll(x, DEPTH - dz, 1), 0.0)
    return jnp.where(z >= -dz, pltpu.roll(x, -dz, 1), 0.0)


def kernel(
    wb_in, wn_in, ab_in, an_in, vel_in, tgt_in, scell_in, swave_in, rcell_in, rtrace_in, w1_in, b1_in, k2_in, b2_in,
    nw_out, nv_out, moves,
    nw, nv, s_out, wb, wn, ab, an, vel, tgt, scell, swave, rcell, rtrace, w1_own, b1, k2_own, b2,
    p0, q0, p1, q1, lap0, lapq, imgacc, vfull, vg, surf, imgt, ra, acca, edge, whole, sides, hb_vel,
    ext, gs, g2, rs, r2, fhi, flo, hid, smat, tt, mask, re, wt, kt,
    s_in, s_hal, r_hal, s_v1, r_v1, s_v2, r_v2, s_hv, r_hv, s_a, r_a, s_b, r_b, s_e, r_e,
):
    shot = lax.axis_index("shot")
    sub = lax.axis_index("sub")
    zh, xc = lax.div(shot, 8), lax.rem(shot, 8)
    zlo, yy = lax.div(sub, 8), lax.rem(sub, 8)
    zz = zh * 2 + zlo
    x0 = sub * ROWS
    up, down = lax.rem(sub + 1, N_SUB), lax.rem(sub + (N_SUB - 1), N_SUB)

    def xc_peer(k):
        return (zh * 8 + lax.rem(xc + k, 8), sub)

    def zh_peer(k):
        return (lax.rem(zh + k, 4) * 8 + xc, sub)

    def z_peer(k):
        z = lax.rem(zz + k, 8)
        return (lax.div(z, 2) * 8 + xc, lax.rem(z, 2) * 8 + yy)

    def y_peer(k):
        return (shot, zlo * 8 + lax.rem(yy + k, 8))

    def near(d, e):
        return (lax.rem(shot + (d + N_SHOT), N_SHOT), lax.rem(sub + (e + N_SUB), N_SUB))

    around = [(d, e) for d in (-1, 0, 1) for e in (-1, 0, 1) if (d, e) != (0, 0)]
    def user(k, d, e):
        owner = lax.rem(zh + k, 4) * 8 + xc
        return (lax.rem(owner + (d + N_SHOT), N_SHOT), lax.rem(sub + (e + N_SUB), N_SUB))

    users = [(k, d, e) for k in (2, 1, 3, 0) for d in (1, -1, 0) for e in (1, -1, 0) if (k, d, e) != (0, 0, 0)]
    twin = (shot, lax.rem(sub + 8, N_SUB))
    greeted = [xc_peer(k) for k in range(1, 8)] + [zh_peer(k) for k in range(1, 4)] + [twin]
    greeted += [near(d, e) for d, e in around]
    loads = [
        pltpu.make_async_copy(outer, inner, s_in.at[n])
        for n, (outer, inner) in enumerate((
            (vel_in, vel), (wn_in, wn), (an_in, an), (wb_in, wb), (ab_in, ab), (rcell_in, rcell),
            (rtrace_in, rtrace), (scell_in, scell), (swave_in, swave), (tgt_in, tgt), (w1_in, w1_own),
            (b1_in, b1), (k2_in, k2_own), (b2_in, b2),
        ))
    ]
    loads[0].start()
    barrier = pltpu.get_barrier_semaphore()
    for device in greeted:
        pl.semaphore_signal(barrier, inc=1, device_id=device, device_id_type=MESH)
    for copy in loads[1:]:
        copy.start()

    pending = []

    def settle(keep=0):
        for copy in pending[: len(pending) - keep]:
            copy.wait_send()
        del pending[: len(pending) - keep]

    def send(src, dst, ssem, rsem, device):
        copy = pltpu.make_async_remote_copy(
            src_ref=src, dst_ref=dst, send_sem=ssem, recv_sem=rsem, device_id=device, device_id_type=MESH
        )
        copy.start()
        pending.append(copy)
        return copy

    loads[0].wait()
    for j in range(2):
        hb_vel[4, j * 8 : (j + 1) * 8, :] = vel[:, j, :]
    own = pl.ds(pl.multiple_of(xc * 16, 16), 16)

    pl.semaphore_wait(barrier, len(greeted))

    every = pl.ds(PAD, COLS)

    def halo(field, index, columns=every):
        return [
            send(
                field.at[pl.ds(8, 4), columns, :], field.at[pl.ds(0, 4), columns, :],
                s_hal.at[index], r_hal.at[index], (shot, up),
            ),
            send(
                field.at[pl.ds(4, 4), columns, :], field.at[pl.ds(12, 4), columns, :],
                s_hal.at[index + 1], r_hal.at[index + 1], (shot, down),
            ),
        ]

    def halo_wait(field, copies):
        for copy in copies:
            copy.wait_recv()

        @pl.when(sub == 0)
        def _():
            field[0:4, PAD : PAD + COLS, :] = jnp.zeros((4, COLS, DEPTH), F32)

        @pl.when(sub == N_SUB - 1)
        def _():
            field[12:16, PAD : PAD + COLS, :] = jnp.zeros((4, COLS, DEPTH), F32)

    behind = (0, 1, 3, 2)
    v1 = [
        send(hb_vel.at[4], vg.at[slot, own, :], s_v1.at[slot - 1], r_v1.at[slot - 1], zh_peer(behind[slot]))
        for slot in (3, 1, 2)
    ]

    vg[0, own, :] = hb_vel[4]

    loads[1].wait()
    p0[4:12, every, :] = wn[0].astype(F32)
    halo_p0 = halo(p0, 0)
    loads[2].wait()
    q0[4:12, every, :] = an[0].astype(F32)
    zeros_pad = jnp.zeros((16, PAD, DEPTH), F32)
    for field in (p0, q0, p1, q1):
        field[:, 0:PAD, :] = zeros_pad
        field[:, PAD + COLS :, :] = zeros_pad

    def around_sends(buffer, ssem, rsem):
        return [
            send(
                buffer.at[4], buffer.at[(1 - d) * 3 + (1 - e)], ssem.at[n], rsem.at[n], near(d, e)
            )
            for n, (d, e) in enumerate(around)
        ]

    for copy in loads[3:9]:
        copy.wait()
    cells = rcell[0].astype(F32)
    hit_y = (
        lax.broadcasted_iota(jnp.int32, (COLS, 256), 0).astype(F32) == jnp.broadcast_to(cells[1:2], (COLS, 256))
    ).astype(F32).astype(BF16)
    rows_here = (lax.broadcasted_iota(jnp.int32, (8, 256), 0) + x0).astype(F32)
    hit_x = (rows_here == jnp.broadcast_to(cells[0:1], (8, 256))).astype(F32)
    trace = jnp.concatenate([hit_x * rtrace[0, 0:1, :], hit_x * rtrace[0, 1:2, :]], axis=0)
    t_hi, t_rest = trace.astype(BF16), trace - trace.astype(BF16).astype(F32)
    t_mid, t_lo = halves(t_rest)
    surf[:, 0:16] = dot_t(hit_y, t_hi) + dot_t(hit_y, t_mid) + dot_t(hit_y, t_lo)

    z_row = lax.broadcasted_iota(jnp.int32, (COLS, DEPTH), 1)
    y_row = lax.broadcasted_iota(jnp.int32, (COLS, DEPTH), 0)
    source_cell = [jnp.broadcast_to(scell[0:1, n : n + 1], (COLS, DEPTH)) for n in range(3)]
    source_yz = (y_row == source_cell[1]) & (z_row == source_cell[2])
    source_amount = [
        jnp.where(source_yz, jnp.broadcast_to(swave[0:1, n : n + 1], (COLS, DEPTH)), 0.0) for n in range(2)
    ]
    rec_mark = z_row == ZREC
    back_w = [None] + [jnp.where(z_row[0:8] >= k, COEFFS[k], 0.0) for k in range(1, 5)]
    fore_w = [None] + [jnp.where(z_row[0:8] < DEPTH - k, COEFFS[k], 0.0) for k in range(1, 5)]

    def tall(w):
        return jnp.broadcast_to(w[0:1], (COLS, DEPTH))

    def lap_row(field, i):
        center = field[i + 4, every, :]
        out = (3.0 * COEFFS[0]) * center
        for k in range(1, 5):
            out = out + COEFFS[k] * (
                (field[i + 4 + k, every, :] + field[i + 4 - k, every, :])
                + (field[i + 4, pl.ds(PAD + k, COLS), :] + field[i + 4, pl.ds(PAD - k, COLS), :])
            )
            out = out + pltpu.roll(center, k, 1) * tall(back_w[k])
            out = out + pltpu.roll(center, DEPTH - k, 1) * tall(fore_w[k])
        return center, out

    def source(i, step):
        return jnp.where(source_cell[0] == x0 + i, source_amount[step], 0.0)

    def receivers(i, step):
        column = pltpu.roll(surf[...], (DEPTH + ZREC - step * 8 - i) % DEPTH, 1)
        return jnp.where(rec_mark, column, 0.0)

    for copy in v1:
        copy.wait_recv()
    v2 = [
        send(vg.at[:, own, :], vg.at[:, own, :], s_v2.at[k - 1], r_v2.at[k - 1], xc_peer(k)) for k in FAR_FIRST
    ]

    halo_q0 = halo(q0, 2)
    halo_wait(p0, halo_p0)

    def forward_0(i, carry):
        center, lap = lap_row(p0, i)
        lap0[i] = lap
        p1[i + 4, every, :] = 2.0 * center - wb[0, i].astype(F32) + source(i, 0)
        return carry

    lax.fori_loop(0, ROWS, forward_0, 0)

    def adjoint_0(i, carry):
        center, lap = lap_row(q0, i)
        lapq[i] = lap
        q1[i + 4, every, :] = 2.0 * center - ab[0, i].astype(F32) + receivers(i, 0)
        return carry

    halo_wait(q0, halo_q0)
    lax.fori_loop(0, ROWS, adjoint_0, 0)

    for copy in v2:
        copy.wait_recv()
    for slot in range(4):
        columns = pl.ds(pl.multiple_of(lax.rem(zh + (4 - behind[slot]), 4) * 16, 16), 16)
        for i in range(ROWS):
            vfull[i, columns, :] = vg.at[slot][pl.ds(i, 16, stride=8), :]
    p1[4:12, every, :] = p1[4:12, every, :] + vfull[...] * lap0[...]
    halo_p1 = halo(p1, 4)
    q1[4:12, every, :] = q1[4:12, every, :] + vfull[...] * lapq[...]
    halo_q1 = halo(q1, 6)

    halo_wait(p1, halo_p1)
    hv = around_sends(hb_vel, s_hv, r_hv)

    def forward_1(i, carry):
        center, lap = lap_row(p1, i)
        fresh = 2.0 * center - p0[i + 4, every, :] + vfull[i] * lap + source(i, 1)
        nw[0, i] = fresh.astype(BF16)
        imgacc[i] = lap * q1[i + 4, every, :]
        return carry

    lax.fori_loop(0, ROWS, forward_1, 0)
    stores = [pltpu.make_async_copy(nw, nw_out, s_out.at[0]), pltpu.make_async_copy(nv, nv_out, s_out.at[1])]
    stores[0].start()

    halo_wait(q1, halo_q1)

    def adjoint_1(i, carry):
        center, lap = lap_row(q1, i)
        fresh = 2.0 * center - q0[i + 4, every, :] + vfull[i] * lap + receivers(i, 1)
        imgacc[i] = imgacc[i] + lap0[i] * fresh
        return carry

    lax.fori_loop(0, ROWS, adjoint_1, 0)
    for z in range(4):
        for i in range(ROWS):
            imgt.at[z][pl.ds(i, 16, stride=8), :] = imgacc[i, z * 16 : (z + 1) * 16, :]

    sends_a = {
        k: send(
            imgt.at[:, pl.ds(pl.multiple_of(lax.rem(xc + k, 8) * 16, 16), 16), :], ra.at[k - 1],
            s_a.at[k - 1], r_a.at[k - 1], xc_peer(k),
        )
        for k in FAR_FIRST
    }
    settle(7)

    for copy in loads[9:]:
        copy.wait()
    lane = lax.broadcasted_iota(jnp.int32, (16, HID), 1)
    tile = lane >> 7
    hid_y = (tile >= 12).astype(jnp.int32) + (tile >= 24).astype(jnp.int32) + (tile >= 36).astype(jnp.int32)
    hid_x = tile - 12 * hid_y
    cell_x = hid_x + (x0 - 1)
    cell_y = hid_y + (2 * shot - 1)
    mask[...] = (
        (hid_x < 10) & (cell_x >= 0) & (cell_x < GRID_X) & (cell_y >= 0) & (cell_y < GRID_Y)
    ).astype(F32)
    gs[...] = jnp.where(lax.broadcasted_iota(jnp.int32, (TILES * 8, DEPTH), 0) % 8 == 6, 1.0, 0.0)
    rs[...] = jnp.zeros((TILES * 8, DEPTH), F32)
    ok_shot = {-1: shot > 0, 0: None, 1: shot < N_SHOT - 1}
    ok_sub = {-1: sub > 0, 0: None, 1: sub < N_SUB - 1}

    def channel(which, piece):
        for d in (-1, 0, 1):
            for e in (-1, 0, 1):
                for j in range(2):
                    block = piece(d, e, j)
                    for ok in (ok_shot[d], ok_sub[e]):
                        if ok is not None:
                            block = block * jnp.where(ok, 1.0, 0.0)
                    row = (2 + 2 * d + j) * WIDE + (0, 2, 10)[e + 1]
                    ext[row : row + block.shape[0], :] = block
        value = ext[...]
        for dz in range(3):
            gs[pl.ds(which * 3 + dz, 72, stride=8), :] = shifted(value, dz - 1)

    def velocity_piece(d, e, j):
        first = j * 8 + (6 if e == -1 else 0)
        block = hb_vel[(d + 1) * 3 + (e + 1), first : first + (8 if e == 0 else 2), :]
        return (block - CENTER_SHIFT) * CENTER_GAIN

    for copy in hv:
        copy.wait_recv()
    channel(1, velocity_piece)

    wt[...] = jnp.zeros((80, DEPTH), F32)
    kt[...] = jnp.zeros((80, DEPTH), F32)
    for n in range(9):
        for i in range(2):
            wt[n * 8 + i * 3 : n * 8 + i * 3 + 3, 0:16] = w1_own[n // 3, n % 3, :, i, :]
        kt[n * 8 : n * 8 + 3, 0:16] = k2_own[n // 3, n % 3, :, 0, :]
    wt[38:39, 0:16] = b1[...]
    w1_hi, w1_lo = halves(wt[:, 0:16])
    k2_hi, k2_lo = halves(kt[:, 0:16])
    unit = (
        lax.broadcasted_iota(jnp.int32, (16, 16), 0) == lax.broadcasted_iota(jnp.int32, (16, 16), 1)
    ).astype(F32).astype(BF16)

    def turn(x):
        return dot_t(unit, x).astype(BF16)

    w1_cat = jnp.concatenate([turn(w1_hi), turn(w1_hi), turn(w1_lo)], axis=1)
    k2_cat = jnp.concatenate([turn(k2_hi), turn(k2_hi), turn(k2_lo)], axis=1)
    k2t_cat = jnp.concatenate([k2_hi, k2_hi, k2_lo], axis=1)

    total = imgt[:, own, :]
    for k in range(1, 8):
        sends_a[k].wait_recv()
        total = total + ra[k - 1]
    acca[...] = total
    for side, first in enumerate((0, 6)):
        for j in range(2):
            edge[side, :, 2 * j : 2 * j + 2, :] = total[:, 8 * j + first : 8 * j + first + 2, :]
    sends_b = []
    for n, (k, d, e) in enumerate(users):
        z = lax.rem(zh + k, 4)
        source_ref = acca.at[z] if e == 0 else edge.at[(e + 1) // 2, z]
        target_ref = whole.at[1 - d, k] if e == 0 else sides.at[(1 - e) // 2, 1 - d, k]
        sends_b.append(send(source_ref, target_ref, s_b.at[n], r_b.at[n], user(k, d, e)))
    whole[1, 0] = acca[zh]
    settle(len(users))
    for copy in sends_b:
        copy.wait_recv()
    image, image_edge = {}, {}
    for d in (-1, 0, 1):
        parts = [whole[d + 1, k] for k in range(4)]
        image[d] = ((parts[0] + parts[1]) + (parts[2] + parts[3])) * (1.0 / N_SHOT)
        for e in (-1, 1):
            parts = [sides[(e + 1) // 2, d + 1, k] for k in range(4)]
            image_edge[d, e] = ((parts[0] + parts[1]) + (parts[2] + parts[3])) * (1.0 / N_SHOT)

    def image_piece(d, e, j):
        if e == 0:
            return image[d][j * 8 : (j + 1) * 8]
        return image_edge[d, e][j * 2 : (j + 1) * 2]

    channel(0, image_piece)

    def spread(source_ref, target_ref):
        for t in range(TILES):
            target_ref[:, t * DEPTH : (t + 1) * DEPTH] = source_ref[t * 8 : (t + 1) * 8, :]

    def stacked(ref, offsets, start):
        parts = [ref[:, start + o * DEPTH : start + o * DEPTH + CHUNK] for o in offsets]
        return jnp.concatenate(parts, axis=0)

    spread(gs, g2)
    for start in range(0, HID, CHUNK):
        here = slice(start, start + CHUNK)
        f_hi, f_lo = halves(stacked(g2, OFFSETS + (0,), start))
        fhi[:, here] = f_hi
        flo[:, here] = f_lo
        pre = dot(w1_cat, jnp.concatenate([f_hi, f_lo, f_hi], axis=0))
        hidden = jnp.tanh(pre) * mask[:, here]
        hid[:, here] = hidden
        h_hi, h_lo = halves(hidden)
        smat[:, here] = dot(k2t_cat, jnp.concatenate([h_hi, h_lo, h_hi], axis=0))

    span = 20 * DEPTH
    turned = smat[0:8, 0:span]
    for n in range(1, 9):
        turned = turned + smat[n * 8 : n * 8 + 8, OFFSETS[n] * DEPTH : OFFSETS[n] * DEPTH + span]
    for t in range(20):
        tt[t * 8 : t * 8 + 8, :] = turned[:, t * DEPTH : (t + 1) * DEPTH]
    bias_sum = jnp.zeros((8, DEPTH), F32)
    for j in range(2):
        update = b2[0]
        for dz in range(3):
            update = update + shifted(tt[pl.ds(j * WIDE * 8 + dz, 8, stride=8), :], dz - 1)
        fresh = hb_vel[4, j * 8 : (j + 1) * 8, :] - update
        nv[:, j, :] = fresh
        slope = tgt[:, j, :] - fresh
        bias_sum = bias_sum + slope
        for dz in range(3):
            rs[pl.ds(((j + 2) * WIDE + 2) * 8 + dz, 8, stride=8), :] = shifted(slope, 1 - dz)

    stores[1].start()

    spread(rs, r2)
    offsets_r = tuple((2 - dy) * WIDE + (2 - dx) for dx in range(3) for dy in range(3)) + (0,)
    grad_1 = jnp.zeros((32, 160), F32)
    grad_2 = jnp.zeros((32, 160), F32)
    for start in range(0, HID, CHUNK):
        here = slice(start, start + CHUNK)
        r_hi, r_lo = halves(stacked(r2, offsets_r, start))
        slope_h = dot(k2_cat, jnp.concatenate([r_hi, r_lo, r_hi], axis=0))
        hidden = hid[:, here]
        h_hi, h_lo = halves(hidden)
        grad_2 = grad_2 + dot_t(jnp.concatenate([h_hi, h_lo], axis=0), jnp.concatenate([r_hi, r_lo], axis=0))
        d_hi, d_lo = halves(slope_h * (1.0 - hidden * hidden) * mask[:, here])
        grad_1 = grad_1 + dot_t(
            jnp.concatenate([d_hi, d_lo], axis=0), jnp.concatenate([fhi[:, here], flo[:, here]], axis=0)
        )

    def joined(grad):
        value = (grad[0:16, 0:80] + grad[0:16, 80:160]) + grad[16:32, 0:80]
        return jnp.concatenate([value, jnp.zeros((16, 48), F32)], axis=1)

    gk1, gk2 = joined(grad_1), joined(grad_2)
    col = lax.broadcasted_iota(jnp.int32, (16, DEPTH), 1)
    row = lax.broadcasted_iota(jnp.int32, (16, DEPTH), 0)
    pack = jnp.where((col < 72) & ((col % 8 < 6) | (col == 38)), gk1, 0.0)
    for n in range(9):
        moved = pltpu.roll(gk2, 72 + 3 * n - 8 * n, 1)
        pack = jnp.where((col >= 72 + 3 * n) & (col < 75 + 3 * n), moved, pack)
    bias = jnp.sum(jnp.sum(bias_sum, axis=0, keepdims=True), axis=1, keepdims=True)
    pack = jnp.where((col == 99) & (row == 0), jnp.broadcast_to(bias, (16, DEPTH)), pack)

    for level, (me, peer) in enumerate(((xc, xc_peer), (zz, z_peer), (yy, y_peer))):
        re[level, me] = pack
        copies = [
            send(
                re.at[level, me], re.at[level, me], s_e.at[level * 7 + k - 1], r_e.at[level * 7 + k - 1], peer(k)
            )
            for k in FAR_FIRST
        ]
        settle(7)
        for copy in copies:
            copy.wait_recv()
        pack = re[level, 0]
        for n in range(1, 8):
            pack = pack + re[level, n]

    squares = jnp.sum(jnp.sum(pack * pack, axis=0, keepdims=True), axis=1, keepdims=True)
    factor = 1.0 / jnp.sqrt(squares * (1.0 / ENTRIES) + 1e-06)
    moves[...] = pack * factor
    for copy in stores:
        copy.wait()

    settle()


def writer(nw, nv, moves, nw_out, nv_out, w1_out, b1_out, k2_out, b2_out, nw_own, nv_own, pack, w1_own, k2_own, sem):
    def copy(source, target, n):
        move = pltpu.make_async_copy(source, target, sem.at[n])
        move.start()
        return move

    loads = [copy(moves, pack, 0), copy(nw, nw_own, 1), copy(nv, nv_own, 2)]
    loads[0].wait()
    turned = jnp.transpose(pack[...])
    for n in range(9):
        for i in range(2):
            w1_own[n // 3, n % 3, :, i, :] = turned[n * 8 + i * 3 : n * 8 + i * 3 + 3]
        k2_own[n // 3, n % 3, :, 0, :] = turned[72 + 3 * n : 75 + 3 * n]
    b1_out[...] = turned[38:39]
    b2_out[...] = pack[0:1, 99:100]
    stores = [copy(w1_own, w1_out, 3), copy(k2_own, k2_out, 4)]
    loads[1].wait()
    stores.append(copy(nw_own, nw_out, 5))
    loads[2].wait()
    stores.append(copy(nv_own, nv_out, 6))
    for move in stores:
        move.wait()


def shards(
    wave_before, wave_now, adjoint_before, adjoint_now, velocity, target_model, source_cell, source_wave,
    receiver_cell, receiver_trace, first_kernel, first_bias, second_kernel, second_bias,
):
    operands = (
        wave_before, wave_now, adjoint_before, adjoint_now, velocity, target_model, source_cell, source_wave,
        receiver_cell.transpose(0, 2, 1), receiver_trace, first_kernel.transpose(2, 3, 4, 1, 0),
        first_bias.reshape(1, 16), second_kernel.transpose(2, 3, 4, 0, 1), second_bias,
    )
    vmem = pl.BlockSpec(memory_space=pltpu.VMEM)
    hbm = pl.BlockSpec(memory_space=pltpu.HBM)
    dma = pltpu.SemaphoreType.DMA
    field = pltpu.VMEM((16, COLS + 2 * PAD, DEPTH), F32)
    block = pltpu.VMEM((ROWS, COLS, DEPTH), F32)
    scratch = [pltpu.VMEM(wave_now.shape, BF16), pltpu.VMEM(velocity.shape, F32), dma((2,))]
    scratch += [pltpu.VMEM(x.shape, x.dtype) for x in operands[:-1]] + [pltpu.SMEM((1,), F32)] + [
        field, field, field, field, block, block, block, block,
        pltpu.VMEM((4, DEPTH, DEPTH), F32),
        pltpu.VMEM((COLS, DEPTH), F32),
        pltpu.VMEM((4, DEPTH, DEPTH), F32),
        pltpu.VMEM((7, 4, 16, DEPTH), F32),
        pltpu.VMEM((4, 16, DEPTH), F32),
        pltpu.VMEM((2, 4, 4, DEPTH), F32),
        pltpu.VMEM((3, 4, 16, DEPTH), F32),
        pltpu.VMEM((2, 3, 4, 4, DEPTH), F32),
        pltpu.VMEM((9, 16, DEPTH), F32),
        pltpu.VMEM((72, DEPTH), F32),
        pltpu.VMEM((TILES * 8, DEPTH), F32),
        pltpu.VMEM((8, TILES * DEPTH), F32),
        pltpu.VMEM((TILES * 8, DEPTH), F32),
        pltpu.VMEM((8, TILES * DEPTH), F32),
        pltpu.VMEM((80, HID), BF16),
        pltpu.VMEM((80, HID), BF16),
        pltpu.VMEM((16, HID), F32),
        pltpu.VMEM((80, HID), F32),
        pltpu.VMEM((160, DEPTH), F32),
        pltpu.VMEM((16, HID), F32),
        pltpu.VMEM((3, 8, 16, DEPTH), F32),
        pltpu.VMEM((80, DEPTH), F32),
        pltpu.VMEM((80, DEPTH), F32),
        dma((len(operands),)),
    ]
    for count in (8, 3, 7, 8, 7, 35, 21):
        scratch += [dma((count,)), dma((count,))]
    next_wave, new_velocity, moves = pl.pallas_call(
        kernel,
        out_shape=(
            jax.ShapeDtypeStruct(wave_now.shape, BF16),
            jax.ShapeDtypeStruct(velocity.shape, F32),
            jax.ShapeDtypeStruct((16, DEPTH), F32),
        ),
        in_specs=[hbm] * len(operands),
        out_specs=(hbm, hbm, vmem),
        scratch_shapes=scratch,
        compiler_params=pltpu.CompilerParams(
            collective_id=0, has_side_effects=True, vmem_limit_bytes=60 * 1024 * 1024
        ),
    )(*operands)
    outs = (
        jax.ShapeDtypeStruct(wave_now.shape, BF16),
        jax.ShapeDtypeStruct(velocity.shape, F32),
        jax.ShapeDtypeStruct((3, 3, 3, 2, 16), F32),
        jax.ShapeDtypeStruct((1, 16), F32),
        jax.ShapeDtypeStruct((3, 3, 3, 1, 16), F32),
        jax.ShapeDtypeStruct((1, 1), F32),
    )
    next_wave, new_velocity, w1, b1, k2, b2 = pl.pallas_call(
        writer,
        out_shape=outs,
        in_specs=[hbm, hbm, hbm],
        out_specs=(hbm, hbm, hbm, vmem, hbm, vmem),
        scratch_shapes=[
            pltpu.VMEM(outs[0].shape, BF16), pltpu.VMEM(outs[1].shape, F32), pltpu.VMEM((16, DEPTH), F32),
            pltpu.VMEM(outs[2].shape, F32), pltpu.VMEM(outs[4].shape, F32), dma((7,)),
        ],
    )(next_wave, new_velocity, moves)
    return (
        next_wave,
        new_velocity,
        w1.transpose(4, 3, 0, 1, 2),
        b1.reshape(16),
        k2.transpose(3, 4, 0, 1, 2),
        b2.reshape(1),
    )


def solution(mesh):
    return jax.shard_map(
        shards,
        mesh=mesh,
        in_specs=(
            P("shot", "sub", None, None),
            P("shot", "sub", None, None),
            P("shot", "sub", None, None),
            P("shot", "sub", None, None),
            P("sub", "shot", None),
            P("sub", "shot", None),
            P("shot", None),
            P("shot", None),
            P("shot", None, None),
            P("shot", None, None),
            P(),
            P(),
            P(),
            P(),
        ),
        out_specs=(P("shot", "sub", None, None), P("sub", "shot", None), P(), P(), P(), P()),
        check_vma=False,
    )
```
